256 devices in a mesh: bricks: 32 (over y, x, core), scenes: 8 (over z).
Axes of the slice: x: 4, y: 4, z: 8, core: 2. Of those that a mesh axis runs over, the one named last changes fastest.
Arguments:
- features: bfloat16 [8, 256, 64, 512], P('scenes', 'bricks'), may hold values from -6 to 6
- cotangent: bfloat16 [8, 256, 64, 512], P('scenes', 'bricks'), may hold values from -6 to 6
- neighbours: int32 [8, 256, 26], P('scenes', 'bricks'), may hold values from -1 to 255, as said below
- mask: int32 [8, 256, 512], P('scenes', 'bricks'), may hold values from 0 to 1, as said below
- weight_one: bfloat16 [64, 1728], replicated, may hold values from -0.15625 to 0.15625
- bias_one: float32 [64], replicated, may hold values from -3 to 3
- weight_two: bfloat16 [64, 1728], replicated, may hold values from -0.15625 to 0.15625
- bias_two: float32 [64], replicated, may hold values from -3 to 3
Outputs:
- output: bfloat16 [8, 256, 64, 512], P('scenes', 'bricks')
- grad_features: bfloat16 [8, 256, 64, 512], P('scenes', 'bricks')
- grad_weight_one: float32 [64, 1728], replicated
- grad_weight_two: float32 [64, 1728], replicated
- grad_bias_one: float32 [64], replicated
- grad_bias_two: float32 [64], replicated
The draws below stay inside these ranges and needn't reach their ends.
Inputs may be any that keep to these rules, and one draw needn't show every extreme that they name: `neighbours`: the bricks are cells of a lattice of 2 x 2 x (2 times the bricks axis's size) cells. Index d of the bricks axis holds the cells with third coordinate in d * 2 .. d * 2 + 1; brick g lies on index g // 8, and its slot s = g % 8 is 2 * 2 x + 2 y + (z - d * 2). Some cells are inactive. Entry j of brick g names the brick at the j-th non-zero offset, or is -1 where that cell is inactive or outside the lattice or where g is inactive. g names h at an offset exactly when h names g at the opposite offset. Inactive bricks have mask 0 on every voxel.
All inputs are finite; a program needn't handle non-finite values.
Results may differ from the reference program's by a relative error of at most 0.015.
Values may be sent and summed in bfloat16 or wider, within the bound.
A program may use at most 128 MiB of HBM per device.

```python
import jax
import jax.numpy as jnp
from jax import lax

C = 64
E = 8
BZ = 2
SCENES = 8
SCENE_BRICKS = 256


def side_offsets():
    offsets = []
    for step_x in (-1, 0, 1):
        for step_y in (-1, 0, 1):
            for step_z in (-1, 0, 1):
                if (step_x, step_y, step_z) != (0, 0, 0):
                    offsets.append((step_x, step_y, step_z))
    return offsets


def lattice_layout():
    bricks_dev = 4 * BZ
    devices = SCENE_BRICKS // bricks_dev
    brick_ids = jnp.arange(SCENE_BRICKS, dtype=jnp.int32)
    owners = brick_ids // bricks_dev
    slot_of = brick_ids % bricks_dev
    pos_x = slot_of // (2 * BZ)
    pos_y = slot_of // BZ % 2
    pos_z = BZ * owners + slot_of % BZ
    extent = (2, 2, BZ * devices)
    return (pos_x, pos_y, pos_z, extent)


def position_ident(pos_x, pos_y, pos_z):
    owners = pos_z // BZ
    slot_of = pos_x * 2 * BZ + pos_y * BZ + pos_z % BZ
    return owners * 4 * BZ + slot_of


def active_bricks(key):
    chance = jax.random.randint(jax.random.fold_in(key, 11), (SCENES, SCENE_BRICKS), 0, 10)
    return chance < 8


def draw_neighbours(key, part):
    active = active_bricks(key)
    pos_x, pos_y, pos_z, extent = lattice_layout()
    entries = []
    for offset in side_offsets():
        next_x = pos_x + offset[0]
        next_y = pos_y + offset[1]
        next_z = pos_z + offset[2]
        inside = (next_x >= 0) & (next_x < extent[0]) & (next_y >= 0) & (next_y < extent[1]) & (next_z >= 0) & (next_z < extent[2])
        target = position_ident(jnp.clip(next_x, 0, extent[0] - 1), jnp.clip(next_y, 0, extent[1] - 1), jnp.clip(next_z, 0, extent[2] - 1))
        entry = jnp.where(inside[None, :] & active & active[:, target], target[None, :], -1)
        entries.append(entry)
    return jnp.stack(entries, axis=-1).astype(jnp.int32)


def draw_mask(key, part):
    active = active_bricks(key)
    key = jax.random.fold_in(key, 2)
    rates = jax.random.randint(jax.random.fold_in(key, 21), (SCENES, SCENE_BRICKS, 1), 3, 10)
    voxels = jax.random.randint(jax.random.fold_in(key, 22), (SCENES, SCENE_BRICKS, E ** 3), 0, 10)
    return ((voxels < rates) & active[:, :, None]).astype(jnp.int32)


def block_levels(key, shape, cuts, low, top_value):
    level, own = 1.0, jax.random.fold_in(key, 6)
    for position, parts in cuts:
        draws = jnp.exp(jax.random.uniform(jax.random.fold_in(own, position), (parts,), jnp.float32, low / len(cuts), top_value / len(cuts)))
        level = level * jnp.repeat(draws, shape[position] // parts).reshape([-1 if axis == position else 1 for axis in range(len(shape))])
    return level


def noise(own_key, shape, width, reach, shards=(), held_as=jnp.bfloat16):
    level = block_levels(own_key, shape, shards, -0.22, 0.18) if shards else 1.0
    drawn = jax.random.normal(own_key, shape, jnp.float32) * width * level
    return jnp.minimum(jnp.maximum(drawn, -reach), reach).astype(held_as)


def setup_inputs(seed: int = 0) -> dict:
    seeds = jax.random.split(jax.random.key(seed), 9)
    return {
        "features": noise(seeds[0], (SCENES, SCENE_BRICKS, C, E ** 3), 1.0, 6.0, ((0, 8), (1, 32))),
        "cotangent": noise(seeds[1], (SCENES, SCENE_BRICKS, C, E ** 3), 1.0, 6.0, ((0, 8), (1, 32))),
        "neighbours": draw_neighbours(jax.random.fold_in(seeds[8], 71), 0),
        "mask": draw_mask(jax.random.fold_in(seeds[8], 71), 0),
        "weight_one": noise(seeds[4], (C, 27 * C), (27 * C) ** -0.5, 0.15625),
        "bias_one": noise(seeds[5], (C,), 0.5, 3.0, (), jnp.float32),
        "weight_two": noise(seeds[6], (C, 27 * C), (27 * C) ** -0.5, 0.15625),
        "bias_two": noise(seeds[7], (C,), 0.5, 3.0, (), jnp.float32),
    }


def tap_list():
    offsets = []
    for step_x in (-1, 0, 1):
        for step_y in (-1, 0, 1):
            for step_z in (-1, 0, 1):
                offsets.append((step_x, step_y, step_z))
    return offsets

def side_list():
    return [offset for offset in tap_list() if offset != (0, 0, 0)]

def brick_faces(cube):
    edge_len = cube.shape[-1]
    return jnp.stack([cube[:, :, 0], cube[:, :, edge_len - 1], cube[:, :, :, 0], cube[:, :, :, edge_len - 1], cube[:, :, :, :, 0], cube[:, :, :, :, edge_len - 1]], axis=1)

def cut_range(step_by, edge_len):
    if step_by == -1:
        return slice(edge_len - 1, edge_len)
    if step_by == 1:
        return slice(0, 1)
    return slice(0, edge_len)

def face_number(offset):
    if offset[0] != 0:
        return 0 if offset[0] == 1 else 1
    if offset[1] != 0:
        return 2 if offset[1] == 1 else 3
    return 4 if offset[2] == 1 else 5

def face_piece(face_rows, offset, edge_len):
    if offset[0] != 0:
        return face_rows[:, :, cut_range(offset[1], edge_len), cut_range(offset[2], edge_len)][:, :, None]
    if offset[1] != 0:
        return face_rows[:, :, :, cut_range(offset[2], edge_len)][:, :, :, None]
    return face_rows[:, :, :, :, None]

def assemble(cube, face_pool, lookup):
    bricks_dev, channels, edge_len = (cube.shape[0], cube.shape[1], cube.shape[2])
    pieces = {(0, 0, 0): cube}
    for number, offset in enumerate(side_list()):
        face_rows = face_pool[lookup[:, number], face_number(offset)]
        pieces[offset] = face_piece(face_rows, offset, edge_len)
    planes = []
    for step_x in (-1, 0, 1):
        row_list = []
        for step_y in (-1, 0, 1):
            row_list.append(jnp.concatenate([pieces[step_x, step_y, step_z] for step_z in (-1, 0, 1)], axis=4))
        planes.append(jnp.concatenate(row_list, axis=3))
    padded = jnp.concatenate(planes, axis=2)
    return padded.reshape(bricks_dev, channels, -1)

def window_conv(padded, weight, edge_len, transpose):
    side_len = edge_len + 2
    start_at = side_len * side_len + side_len + 1
    length = (edge_len - 1) * start_at + 1
    channels = weight.shape[0]
    totals = jnp.zeros((padded.shape[0], channels, length), jnp.float32)
    for number, offset in enumerate(tap_list()):
        shift_by = offset[0] * side_len * side_len + offset[1] * side_len + offset[2]
        kernel = weight[:, number * channels:(number + 1) * channels].astype(jnp.float32)
        if transpose:
            window = padded[:, :, start_at - shift_by:start_at - shift_by + length].astype(jnp.float32)
            totals = totals + jnp.einsum('oi,bop->bip', kernel, window, precision=lax.Precision.HIGHEST)
        else:
            window = padded[:, :, start_at + shift_by:start_at + shift_by + length].astype(jnp.float32)
            totals = totals + jnp.einsum('oi,bip->bop', kernel, window, precision=lax.Precision.HIGHEST)
    return totals

def interior(window, edge_len):
    side_len = edge_len + 2
    start_at = side_len * side_len + side_len + 1
    bricks_dev, channels = (window.shape[0], window.shape[1])
    zero_fill = jnp.zeros((bricks_dev, channels, start_at), window.dtype)
    full_grid = jnp.concatenate([zero_fill, window, zero_fill], axis=2).reshape(bricks_dev, channels, side_len, side_len, side_len)
    return full_grid[:, :, 1:edge_len + 1, 1:edge_len + 1, 1:edge_len + 1].reshape(bricks_dev, channels, -1)

def placed(values, edge_len):
    side_len = edge_len + 2
    start_at = side_len * side_len + side_len + 1
    length = (edge_len - 1) * start_at + 1
    bricks_dev, channels = (values.shape[0], values.shape[1])
    cube_all = values.reshape(bricks_dev, channels, edge_len, edge_len, edge_len)
    full_grid = jnp.pad(cube_all, ((0, 0), (0, 0), (1, 1), (1, 1), (1, 1))).reshape(bricks_dev, channels, -1)
    return full_grid[:, :, start_at:start_at + length]

def weight_grad(window, padded, edge_len):
    side_len = edge_len + 2
    start_at = side_len * side_len + side_len + 1
    length = (edge_len - 1) * start_at + 1
    window_f = window.astype(jnp.float32)
    partial_value = []
    for offset in tap_list():
        shift_by = offset[0] * side_len * side_len + offset[1] * side_len + offset[2]
        source = padded[:, :, start_at + shift_by:start_at + shift_by + length].astype(jnp.float32)
        partial_value.append(jnp.einsum('bop,bip->oi', window_f, source, precision=lax.Precision.HIGHEST))
    return jnp.concatenate(partial_value, axis=1)

def silu_slope(values):
    sigma = jax.nn.sigmoid(values)
    return sigma * (1.0 + values * (1.0 - sigma))

def scene_pass(features, cotangent, neighbours, mask, weight_one, bias_one, weight_two, bias_two):
    bricks_all, channels = (features.shape[0], features.shape[1])
    live_mask = mask.astype(jnp.float32)[:, None, :]
    masked = features * mask.astype(features.dtype)[:, None, :]
    lookup = jnp.where(neighbours >= 0, neighbours, bricks_all).astype(jnp.int32)

    def pad_all(values):
        cube_all = values.reshape(bricks_all, channels, E, E, E)
        face_pool = jnp.concatenate([brick_faces(cube_all), jnp.zeros((1, 6, channels, E, E), values.dtype)], axis=0)
        return assemble(cube_all, face_pool, lookup)
    masked_pad = pad_all(masked)
    first = live_mask * (interior(window_conv(masked_pad, weight_one, E, False), E) + bias_one[None, :, None])
    hidden = jax.nn.silu(first).astype(jnp.bfloat16)
    hidden_pad = pad_all(hidden)
    second = live_mask * (interior(window_conv(hidden_pad, weight_two, E, False), E) + bias_two[None, :, None])
    summed = second + masked.astype(jnp.float32)
    output = jax.nn.silu(summed).astype(jnp.bfloat16)
    grad_summed = (cotangent.astype(jnp.float32) * silu_slope(summed) * live_mask).astype(jnp.bfloat16)
    grad_pad = pad_all(grad_summed)
    grad_weight_two = weight_grad(placed(grad_summed, E), hidden_pad, E)
    grad_bias_two = lax.optimization_barrier(jnp.sum(grad_summed.astype(jnp.float32), axis=(0, 2)))
    grad_first = (interior(window_conv(grad_pad, weight_two, E, True), E) * silu_slope(first) * live_mask).astype(jnp.bfloat16)
    first_pad = pad_all(grad_first)
    grad_weight_one = weight_grad(placed(grad_first, E), masked_pad, E)
    grad_bias_one = lax.optimization_barrier(jnp.sum(grad_first.astype(jnp.float32), axis=(0, 2)))
    grad_features = (live_mask * (grad_summed.astype(jnp.float32) + interior(window_conv(first_pad, weight_one, E, True), E))).astype(jnp.bfloat16)
    return (output, grad_features, grad_weight_one, grad_weight_two, grad_bias_one, grad_bias_two)

def reference(features, cotangent, neighbours, mask, weight_one, bias_one, weight_two, bias_two):

    def one_scene(items):
        return scene_pass(items[0], items[1], items[2], items[3], weight_one, bias_one, weight_two, bias_two)
    results = lax.map(one_scene, (features, cotangent, neighbours, mask))
    return (results[0], results[1], lax.optimization_barrier(jnp.sum(results[2], axis=0)), lax.optimization_barrier(jnp.sum(results[3], axis=0)), lax.optimization_barrier(jnp.sum(results[4], axis=0)), lax.optimization_barrier(jnp.sum(results[5], axis=0)))
```

```python
import functools

import jax
import jax.numpy as jnp
from jax import lax
from jax.experimental import pallas as pl
from jax.experimental.pallas import tpu as pltpu
from jax.sharding import PartitionSpec as P

C = 64
E = 8
S = 16
PL = S * S
L = 128
HALF = 512
BIAS_ROW = 864 - HALF
F32 = jnp.float32
BF16 = jnp.bfloat16


def dot_nn(a, b):
    return lax.dot_general(a, b, (((1,), (0,)), ((), ())), preferred_element_type=F32)


def dot_nt(a, b):
    return lax.dot_general(a, b, (((1,), (1,)), ((), ())), preferred_element_type=F32)


def eye(rows, cols):
    r = lax.broadcasted_iota(jnp.int32, (rows, cols), 0)
    c = lax.broadcasted_iota(jnp.int32, (rows, cols), 1)
    return jnp.where(r == c, 1.0, 0.0).astype(BF16)


def low_lanes(rows):
    return lax.broadcasted_iota(jnp.int32, (rows, L), 1) < C


def tap_of(dx, dy, dz):
    return 9 * (dx + 1) + 3 * (dy + 1) + (dz + 1)


def copy_to(src, dst, send, recv, device):
    return pltpu.make_async_remote_copy(
        src_ref=src,
        dst_ref=dst,
        send_sem=send,
        recv_sem=recv,
        device_id=device,
        device_id_type=pl.DeviceIdType.MESH,
    )


def sigmoid(v):
    return 1.0 / (1.0 + jnp.exp(-v))


def kernel(
    nb,
    ns,
    feat,
    cot,
    mask,
    w1,
    b1,
    w2,
    b2,
    out,
    gfeat,
    gw1,
    gw2,
    gb1,
    gb2,
    f0,
    f1,
    f2,
    yy,
    gt,
    u0,
    mm,
    ct,
    us,
    sl,
    gs,
    oo,
    wt,
    wd,
    wa,
    halo_out,
    halo_in,
    halo_wide,
    grads,
    pack,
    part1,
    sum1,
    part2,
    sum2,
    part3,
    sum3,
    full,
    halo_send,
    halo_recv,
    pair_send,
    pair_recv,
    chip_send,
    chip_recv,
    scene_send,
    scene_recv,
):
    nq = nb // 2
    b = lax.axis_index("bricks")
    s = lax.axis_index("scenes")
    core = lax.rem(b, 2)
    q = b // 2
    below = lax.rem(b + nb - 1, nb)
    above = lax.rem(b + 1, nb)
    other = b + 1 - 2 * core

    def chip_at(j):
        return {"bricks": 2 * lax.rem(q + j, nq) + core}

    def scene_at(j):
        return {"scenes": lax.rem(s + j, ns)}

    barrier = pltpu.get_barrier_semaphore()

    def greet(device):
        pl.semaphore_signal(barrier, inc=1, device_id=device, device_id_type=pl.DeviceIdType.MESH)

    greet({"bricks": below})
    greet({"bricks": above})
    lax.fori_loop(1, nq, lambda j, c: (greet(chip_at(j)), c)[1], 0)
    lax.fori_loop(1, ns, lambda j, c: (greet(scene_at(j)), c)[1], 0)

    eye256 = eye(PL, PL)
    eye128 = eye(L, L)
    eye64 = eye(C, C)
    eye64w = eye(C, L)

    def load_features(column, carry):
        bx, by = column // 2, lax.rem(column, 2)
        for bz in range(2):
            n = column * 2 + bz
            live = mask[0, pl.ds(n, 1), :].astype(F32)
            live = jnp.broadcast_to(live, (L, 2 * PL)).astype(BF16)
            masked = feat[0, n] * live[:C]
            for h in range(2):
                cols = slice(h * PL, (h + 1) * PL)
                stack = jnp.concatenate([masked[:, cols], masked[:, cols], live[:, cols]], axis=0)
                turned = dot_nt(eye256, stack)
                place = (pl.ds(bx * E + 4 * h, 4), pl.ds(by * E, E), slice(bz * E, bz * E + E))
                u0[place] = turned[:, :L].reshape(4, E, E, L)
                mm[place] = turned[:, L:].reshape(4, E, E, L)
        return carry

    def load_cotangent(column, carry):
        bx, by = column // 2, lax.rem(column, 2)
        for bz in range(2):
            value = cot[0, column * 2 + bz]
            for h in range(2):
                cols = slice(h * PL, (h + 1) * PL)
                stack = jnp.concatenate([value[:, cols], value[:, cols]], axis=0)
                place = (pl.ds(bx * E + 4 * h, 4), pl.ds(by * E, E), slice(bz * E, bz * E + E))
                ct[place] = dot_nt(eye256, stack).reshape(4, E, E, L)
        return carry

    def store_bricks(target):
        for n in range(8):
            bx, by, bz = n // 4, n // 2 % 2, n % 2
            rows = oo[bx * E : bx * E + E, by * E : by * E + E, bz * E : bz * E + E, :]
            rows = rows.reshape(E * E * E, L).astype(BF16)
            target[0, n] = dot_nt(eye64w, rows).astype(BF16)

    def prepare_weights(w, number, forward):
        spread = jnp.concatenate([eye64, eye64], axis=1)
        for m in range(14):
            size = L if m < 13 else C
            tile = w[:, m * L : m * L + size]
            if forward:
                twice = jnp.concatenate([tile, tile], axis=0)
                wt[m * L : m * L + size, :] = dot_nt(eye128 if m < 13 else eye64, twice)
            else:
                for part in range(size // C):
                    zeros = jnp.zeros((C, L), BF16)
                    if m == 13:
                        select = spread
                    else:
                        select = jnp.concatenate([spread, zeros] if part == 0 else [zeros, spread], axis=0)
                    k = 2 * m + part
                    wd[k * C : k * C + C, :] = dot_nn(tile, select)
        low = low_lanes(C)
        for dy in (-1, 0, 1):
            for i, dz in enumerate((-1, 0, 1)):

                def block(dx):
                    if forward:
                        k = tap_of(dx, dy, dz)
                        return wt[k * C : k * C + C, :]
                    k = tap_of(-dx, -dy, -dz)
                    return wd[k * C : k * C + C, :]

                rows = slice((dy + 1) * PL + i * C, (dy + 1) * PL + i * C + C)
                wa[number, rows, :L] = jnp.where(low, block(-1), block(1)).astype(BF16)
                wa[number, rows, L:] = block(0).astype(BF16)
            wa[number, (dy + 1) * PL + 3 * C : (dy + 2) * PL, :] = jnp.zeros((C, PL), BF16)

    low_half = low_lanes(PL // 2)

    def halo_copy(field, way):
        return copy_to(
            halo_out.at[field, way],
            halo_in.at[field, way],
            halo_send.at[field, way],
            halo_recv.at[field, way],
            {"bricks": above if way == 0 else below},
        )

    def send_halo(field):
        for way, z in ((0, S - 1), (1, 0)):
            plane = us[pl.ds(z, PL, stride=S), :]
            packed = jnp.where(low_half, plane[: PL // 2], plane[PL // 2 :])
            halo_out[field, way] = packed.astype(BF16)
            halo_copy(field, way).start()

    def receive_halo(field):
        for way in range(2):
            halo_copy(field, way).wait()
            got = halo_in[field, way].astype(F32)
            exists = (b > 0) if way == 0 else (b < nb - 1)
            got = got * jnp.where(exists, 1.0, 0.0)
            swapped = pltpu.roll(got, C, 1)
            halo_wide[way, : PL // 2, :] = jnp.where(low_half, got, swapped)
            halo_wide[way, PL // 2 :, :] = jnp.where(low_half, swapped, got)

    low_plane = low_lanes(PL)
    z_of = lax.broadcasted_iota(jnp.int32, (PL, L), 0) & (S - 1)

    def rows_of(x):
        return pl.ds(pl.multiple_of(x * PL, PL), PL)

    def fill(field):
        def step(x, carry):
            u = us[rows_of(x), :]
            at = pl.ds(pl.multiple_of(x * S, S), S)
            low_z = jnp.broadcast_to(halo_wide[0, at, :][:, None, :], (S, S, L)).reshape(PL, L)
            high_z = jnp.broadcast_to(halo_wide[1, at, :][:, None, :], (S, S, L)).reshape(PL, L)
            down = jnp.where(z_of == 0, low_z, pltpu.roll(u, 1, 0))
            up = jnp.where(z_of == S - 1, high_z, pltpu.roll(u, PL - 1, 0))
            tile = jnp.where(low_plane, down, u)
            field[x, 1 : S + 1, :, :L] = tile.reshape(S, S, L).astype(BF16)
            field[x, 1 : S + 1, :, L:] = up.reshape(S, S, L).astype(BF16)
            return carry

        lax.fori_loop(0, S, step, 0)

    def conv(field, number, first, last):
        def step(x, carry):
            rows = jnp.concatenate([field[x, e : e + S].reshape(PL, PL) for e in range(3)], axis=1)
            yy[x + 1] = dot_nn(rows, wa[number])
            return carry

        lax.fori_loop(first, last, step, 0)

    def conv_result(x):
        sides = jnp.where(low_plane, yy[x, :, :L], yy[x + 2, :, :L])
        return sides + pltpu.roll(sides, C, 1) + yy[x + 1, :, L:]

    def turn(x, value):
        gt[pl.ds(pl.multiple_of((x + 1) * C, C), C), :] = dot_nt(eye64w, value).astype(BF16)

    def weight_grad(field, number):
        grads[...] = jnp.zeros((3, 3 * C, PL), F32)

        def step(i, carry):
            left = jnp.concatenate(
                [gt[pl.ds(pl.multiple_of((4 * i + p) * C, C), 3 * C), :] for p in range(4)], axis=1
            )
            for e in range(3):
                right = field[pl.ds(4 * i, 4), e : e + S].reshape(4 * PL, PL)
                grads[e] += dot_nn(left, right)
            return carry

        lax.fori_loop(0, S // 4, step, 0)
        low = low_lanes(96)
        for e in range(3):
            for j in range(3):
                row = e * 3 * C + j * C
                pack[number, row // HALF, row % HALF : row % HALF + C, :] = grads[e, j * C : j * C + C, :L]
            row = 9 * C + e * 96 - HALF
            pack[number, 1, row : row + 96, :] = jnp.where(low, grads[e, :96, L:], grads[e, 96:, L:])

    def pack_bias(number, total):
        row = jnp.sum(total, axis=0, keepdims=True)
        pack[number, 1, BIAS_ROW : BIAS_ROW + 8, :] = jnp.broadcast_to(row, (8, L))

    def unpack(number, weight, bias):
        low = low_lanes(C)

        def piece(k):
            dx, dy, dz = k // 9, k // 3 % 3, k % 3
            j = 2 - dx
            if dz < 2:
                row = dy * 3 * C + j * C
                return packed(number, row, C), dz
            base = 9 * C + dy * 96
            if j == 0:
                return packed(number, base, C), 0
            if j == 2:
                return packed(number, base + 32, C), 1
            first = packed(number, base + 64, 32)
            second = pltpu.roll(packed(number, base, 32), C, 1)
            return jnp.concatenate([first, second], axis=0), 0

        def placed(k, half):
            value, at = piece(k)
            return value if at == half else pltpu.roll(value, C, 1)

        for m in range(13):
            weight[:, m * L : m * L + L] = jnp.where(low, placed(2 * m, 0), placed(2 * m + 1, 1))
        weight[:, 13 * L :] = placed(26, 0)[:, :C]
        bias[...] = full[number, 1, BIAS_ROW // chunk, BIAS_ROW % chunk : BIAS_ROW % chunk + 1, :C]

    chunk = HALF // nq

    def packed(number, row, size):
        half, at = row // HALF, row % HALF
        return full[number, half].reshape(HALF, L)[at : at + size]

    def pair_copy(number, step):
        if step == 0:
            src, dst = pack.at[number, 1 - core], part1.at[number]
        else:
            src, dst = full.at[number, core], full.at[number, core]
        return copy_to(src, dst, pair_send.at[number, step], pair_recv.at[number, step], {"bricks": other})

    def reduce_chips_copy(number, j):
        return copy_to(
            sum1.at[number, lax.rem(q + j, nq)],
            part2.at[number, j],
            chip_send.at[number, 0, j],
            chip_recv.at[number, 0, j],
            chip_at(j),
        )

    def scene_copy(number, j, sender):
        return copy_to(
            sum2.at[number],
            part3.at[number, sender],
            scene_send.at[number, j],
            scene_recv.at[number, j],
            scene_at(j),
        )

    def gather_chips_copy(number, j, sender):
        return copy_to(
            sum3.at[number],
            full.at[number, core, sender],
            chip_send.at[number, 1, j],
            chip_recv.at[number, 1, j],
            chip_at(j),
        )

    def each(count, act):
        def step(j, carry):
            act(j)
            return carry

        lax.fori_loop(1, count, step, 0)

    def sum_start(number):
        pair_copy(number, 0).start()

    def sum_chips(number):
        pair_copy(number, 0).wait()
        total = pack[number, core] + part1[number]
        sum1[number] = total.reshape(nq, chunk, L)
        each(nq, lambda j: reduce_chips_copy(number, j).start())

    def sum_scenes(number):
        each(nq, lambda j: reduce_chips_copy(number, j).wait())
        total = sum1[number, q]
        for j in range(1, nq):
            total += part2[number, j]
        sum2[number] = total
        part3[number, s] = total
        each(ns, lambda j: scene_copy(number, j, s).start())

    def gather_chips(number):
        each(ns, lambda j: scene_copy(number, j, lax.rem(s + ns - j, ns)).wait())
        total = part3[number, 0]
        for j in range(1, ns):
            total += part3[number, j]
        sum3[number] = total
        full[number, core, q] = total
        each(nq, lambda j: gather_chips_copy(number, j, q).start())

    def gather_pair(number):
        each(nq, lambda j: gather_chips_copy(number, j, lax.rem(q + nq - j, nq)).wait())
        pair_copy(number, 1).start()

    def sum_end(number):
        pair_copy(number, 1).wait()

    for field in (f0, f1, f2):
        field[:, 0] = jnp.zeros((S, S, PL), BF16)
        field[:, S + 1] = jnp.zeros((S, S, PL), BF16)
    yy[0] = jnp.zeros((PL, PL), F32)
    yy[S + 1] = jnp.zeros((PL, PL), F32)
    gt[:C] = jnp.zeros((C, PL), BF16)
    gt[(S + 1) * C :] = jnp.zeros((C, PL), BF16)
    for number in range(2):
        pack[number, 1, BIAS_ROW:, :] = jnp.zeros((HALF - BIAS_ROW, L), F32)

    lax.fori_loop(0, 4, load_features, 0)

    def copy_in(x, carry):
        us[rows_of(x), :] = u0[x].reshape(PL, L)
        return carry

    lax.fori_loop(0, S, copy_in, 0)
    pl.semaphore_wait(barrier, 2 + (nq - 1) + (ns - 1))
    send_halo(0)
    prepare_weights(w1, 0, True)
    receive_halo(0)
    fill(f0)
    conv(f0, 0, 0, S)

    def after_first(x, carry):
        live = mm[x].reshape(PL, L)
        bias = jnp.concatenate([b1[...], b1[...]], axis=1)
        first = live * (conv_result(x) + bias)
        sig = sigmoid(first)
        hidden = first * sig
        sl[rows_of(x), :] = live * (sig + hidden * (1.0 - sig))
        us[rows_of(x), :] = hidden.astype(BF16).astype(F32)
        return carry

    lax.fori_loop(0, S, after_first, 0)
    send_halo(1)
    prepare_weights(w2, 1, True)
    prepare_weights(w2, 2, False)
    prepare_weights(w1, 3, False)
    lax.fori_loop(0, 4, load_cotangent, 0)
    receive_halo(1)
    fill(f1)
    conv(f1, 1, 0, S)

    def after_second(x, carry):
        live = mm[x].reshape(PL, L)
        bias = jnp.concatenate([b2[...], b2[...]], axis=1)
        summed = live * (conv_result(x) + bias) + u0[x].reshape(PL, L)
        sig = sigmoid(summed)
        value = summed * sig
        oo[x] = value.reshape(S, S, L)
        slope = sig + value * (1.0 - sig)
        grad = (ct[x].reshape(PL, L) * slope * live).astype(BF16)
        turn(x, grad)
        grad = grad.astype(F32)
        us[rows_of(x), :] = grad
        gs[rows_of(x), :] = grad
        return carry + jnp.sum(grad.reshape(PL // 8, 8, L), axis=0)

    total = lax.fori_loop(0, S, after_second, jnp.zeros((8, L), F32))
    send_halo(2)
    pack_bias(1, total)
    weight_grad(f1, 1)
    sum_start(1)
    store_bricks(out)
    receive_halo(2)
    fill(f2)
    sum_chips(1)
    conv(f2, 2, 0, S)
    sum_scenes(1)

    def after_third(x, carry):
        grad = (conv_result(x) * sl[rows_of(x), :]).astype(BF16)
        turn(x, grad)
        grad = grad.astype(F32)
        us[rows_of(x), :] = grad
        return carry + jnp.sum(grad.reshape(PL // 8, 8, L), axis=0)

    total = lax.fori_loop(0, S, after_third, jnp.zeros((8, L), F32))
    send_halo(3)
    gather_chips(1)
    pack_bias(0, total)
    weight_grad(f0, 0)
    sum_start(0)
    gather_pair(1)
    receive_halo(3)
    fill(f2)
    sum_chips(0)
    conv(f2, 3, 0, S)
    sum_scenes(0)
    sum_end(1)

    def after_fourth(x, carry):
        value = mm[x].reshape(PL, L) * (gs[rows_of(x), :] + conv_result(x))
        oo[x] = value.reshape(S, S, L)
        return carry

    lax.fori_loop(0, S, after_fourth, 0)
    gather_chips(0)
    store_bricks(gfeat)
    gather_pair(0)
    unpack(1, gw2, gb2)
    sum_end(0)
    unpack(0, gw1, gb1)


def local(nb, ns, features, cotangent, mask, w1, b1, w2, b2):
    nq = nb // 2
    chunk = HALF // nq
    vmem = pltpu.VMEM
    field = vmem((S, S + 2, S, PL), BF16)
    block4 = vmem((S, S, S, L), F32)
    block2 = vmem((S * PL, L), F32)
    dma = pltpu.SemaphoreType.DMA
    scratch = [
        field,
        field,
        field,
        vmem((S + 2, PL, PL), F32),
        vmem(((S + 2) * C, PL), BF16),
        block4,
        block4,
        block4,
        block2,
        block2,
        block2,
        block4,
        vmem((27 * C, L), F32),
        vmem((27 * C, L), F32),
        vmem((4, 3 * PL, PL), BF16),
        vmem((4, 2, PL // 2, L), BF16),
        vmem((4, 2, PL // 2, L), BF16),
        vmem((2, PL, L), F32),
        vmem((3, 3 * C, PL), F32),
        vmem((2, 2, HALF, L), F32),
        vmem((2, HALF, L), F32),
        vmem((2, nq, chunk, L), F32),
        vmem((2, nq, chunk, L), F32),
        vmem((2, chunk, L), F32),
        vmem((2, ns, chunk, L), F32),
        vmem((2, chunk, L), F32),
        vmem((2, 2, nq, chunk, L), F32),
        dma((4, 2)),
        dma((4, 2)),
        dma((2, 2)),
        dma((2, 2)),
        dma((2, 2, nq)),
        dma((2, 2, nq)),
        dma((2, ns)),
        dma((2, ns)),
    ]
    shape = jax.ShapeDtypeStruct
    in_vmem = pl.BlockSpec(memory_space=pltpu.VMEM)
    output, grad_features, gw1, gw2, gb1, gb2 = pl.pallas_call(
        functools.partial(kernel, nb, ns),
        out_shape=[
            shape(features.shape, BF16),
            shape(features.shape, BF16),
            shape(w1.shape, F32),
            shape(w2.shape, F32),
            shape((1, C), F32),
            shape((1, C), F32),
        ],
        in_specs=[in_vmem] * 7,
        out_specs=[in_vmem] * 6,
        scratch_shapes=scratch,
        compiler_params=pltpu.CompilerParams(
            collective_id=0, has_side_effects=True, vmem_limit_bytes=56 * 1024 * 1024
        ),
        name="residual_block",
    )(features, cotangent, mask, w1, b1.reshape(1, C), w2, b2.reshape(1, C))
    return output, grad_features, gw1, gw2, gb1.reshape(C), gb2.reshape(C)


def solution(mesh):
    nb, ns = mesh.shape["bricks"], mesh.shape["scenes"]

    def program(features, cotangent, neighbours, mask, weight_one, bias_one, weight_two, bias_two):
        del neighbours
        split = P("scenes", "bricks", None, None)
        return jax.shard_map(
            functools.partial(local, nb, ns),
            mesh=mesh,
            in_specs=(split, split, P("scenes", "bricks", None), P(), P(), P(), P()),
            out_specs=(split, split, P(), P(), P(), P()),
            check_vma=False,
        )(features, cotangent, mask, weight_one, bias_one, weight_two, bias_two)

    return program
```

```python
import functools

import jax
import jax.numpy as jnp
from jax import lax
from jax.experimental import pallas as pl
from jax.experimental.pallas import tpu as pltpu
from jax.sharding import PartitionSpec as P

C = 64
E = 8
S = 16
PL = S * S
L = 128
HALF = 512
BIAS_ROW = 864 - HALF
F32 = jnp.float32
BF16 = jnp.bfloat16


def dot_nn(a, b):
    return lax.dot_general(a, b, (((1,), (0,)), ((), ())), preferred_element_type=F32)


def dot_nt(a, b):
    return lax.dot_general(a, b, (((1,), (1,)), ((), ())), preferred_element_type=F32)


def eye(rows, cols):
    r = lax.broadcasted_iota(jnp.int32, (rows, cols), 0)
    c = lax.broadcasted_iota(jnp.int32, (rows, cols), 1)
    return jnp.where(r == c, 1.0, 0.0).astype(BF16)


def low_lanes(rows):
    return lax.broadcasted_iota(jnp.int32, (rows, L), 1) < C


def tap_of(dx, dy, dz):
    return 9 * (dx + 1) + 3 * (dy + 1) + (dz + 1)


def copy_to(src, dst, send, recv, device):
    return pltpu.make_async_remote_copy(
        src_ref=src,
        dst_ref=dst,
        send_sem=send,
        recv_sem=recv,
        device_id=device,
        device_id_type=pl.DeviceIdType.MESH,
    )


def sigmoid(v):
    return 1.0 / (1.0 + jnp.exp(-v))


def kernel(
    nb,
    ns,
    feat,
    cot_hbm,
    mask,
    w1,
    b1,
    w2_hbm,
    b2,
    out,
    gfeat,
    sums,
    cot,
    w2,
    f0,
    f1,
    f2,
    yy,
    gt,
    u0,
    mm,
    ct,
    us,
    sl,
    gs,
    oo,
    o2,
    wt,
    wd,
    wa,
    halo_out,
    halo_in,
    halo_wide,
    grads,
    pack,
    part1,
    sum1,
    part2,
    sum2,
    part3,
    sum3,
    full,
    halo_send,
    halo_recv,
    pair_send,
    pair_recv,
    chip_send,
    chip_recv,
    scene_send,
    scene_recv,
    load_sem,
):
    nq = nb // 2
    b = lax.axis_index("bricks")
    s = lax.axis_index("scenes")
    core = lax.rem(b, 2)
    q = b // 2
    below = lax.rem(b + nb - 1, nb)
    above = lax.rem(b + 1, nb)
    other = b + 1 - 2 * core

    def chip_at(j):
        return {"bricks": 2 * lax.rem(q + j, nq) + core}

    def scene_at(j):
        return {"scenes": lax.rem(s + j, ns)}

    cot_load = pltpu.make_async_copy(cot_hbm, cot, load_sem.at[0])
    w2_load = pltpu.make_async_copy(w2_hbm, w2, load_sem.at[1])
    cot_load.start()
    w2_load.start()

    barrier = pltpu.get_barrier_semaphore()

    def greet(device):
        pl.semaphore_signal(barrier, inc=1, device_id=device, device_id_type=pl.DeviceIdType.MESH)

    greet({"bricks": below})
    greet({"bricks": above})
    for j in range(1, nq):
        greet(chip_at(j))
    for j in range(1, ns):
        greet(scene_at(j))

    eye256 = eye(PL, PL)
    eye128 = eye(L, L)
    eye64 = eye(C, C)
    eye64w = eye(C, L)

    def load_features(column):
        bx, by = column // 2, column % 2
        for bz in range(2):
            n = column * 2 + bz
            live = mask[0, n : n + 1, :].astype(F32)
            live = jnp.broadcast_to(live, (L, 2 * PL)).astype(BF16)
            masked = feat[0, n] * live[:C]
            for h in range(2):
                cols = slice(h * PL, (h + 1) * PL)
                stack = jnp.concatenate([masked[:, cols], masked[:, cols], live[:, cols]], axis=0)
                turned = dot_nt(eye256, stack)
                x, y, z = bx * E + 4 * h, by * E, bz * E
                place = (slice(x, x + 4), slice(y, y + E), slice(z, z + E))
                u0[place] = turned[:, :L].reshape(4, E, E, L)
                mm[place] = turned[:, L:].reshape(4, E, E, L)

    def load_cotangent(column):
        bx, by = column // 2, column % 2
        for bz in range(2):
            value = cot[0, column * 2 + bz]
            for h in range(2):
                cols = slice(h * PL, (h + 1) * PL)
                stack = jnp.concatenate([value[:, cols], value[:, cols]], axis=0)
                x, y, z = bx * E + 4 * h, by * E, bz * E
                place = (slice(x, x + 4), slice(y, y + E), slice(z, z + E))
                ct[place] = dot_nt(eye256, stack).reshape(4, E, E, L)

    def store_bricks(oo, target):
        for n in range(8):
            bx, by, bz = n // 4, n // 2 % 2, n % 2
            rows = oo[bx * E : bx * E + E, by * E : by * E + E, bz * E : bz * E + E, :]
            rows = rows.reshape(E * E * E, L).astype(BF16)
            target[0, n] = dot_nt(eye64w, rows).astype(BF16)

    def prepare_weights(w, number, forward):
        spread = jnp.concatenate([eye64, eye64], axis=1)
        for m in range(14):
            size = L if m < 13 else C
            tile = w[:, m * L : m * L + size]
            if forward:
                twice = jnp.concatenate([tile, tile], axis=0)
                wt[m * L : m * L + size, :] = dot_nt(eye128 if m < 13 else eye64, twice)
            else:
                for part in range(size // C):
                    zeros = jnp.zeros((C, L), BF16)
                    if m == 13:
                        select = spread
                    else:
                        select = jnp.concatenate([spread, zeros] if part == 0 else [zeros, spread], axis=0)
                    k = 2 * m + part
                    wd[k * C : k * C + C, :] = dot_nn(tile, select)
        low = low_lanes(C)
        for dy in (-1, 0, 1):
            for i, dz in enumerate((-1, 0, 1)):

                def block(dx):
                    if forward:
                        k = tap_of(dx, dy, dz)
                        return wt[k * C : k * C + C, :]
                    k = tap_of(-dx, -dy, -dz)
                    return wd[k * C : k * C + C, :]

                rows = slice((dy + 1) * PL + i * C, (dy + 1) * PL + i * C + C)
                wa[number, rows, :L] = jnp.where(low, block(-1), block(1)).astype(BF16)
                wa[number, rows, L:] = block(0).astype(BF16)
            wa[number, (dy + 1) * PL + 3 * C : (dy + 2) * PL, :] = jnp.zeros((C, PL), BF16)

    low_half = low_lanes(PL // 2)

    def halo_copy(field, way):
        return copy_to(
            halo_out.at[field, way],
            halo_in.at[field, way],
            halo_send.at[field, way],
            halo_recv.at[field, way],
            {"bricks": above if way == 0 else below},
        )

    def send_halo(field):
        for way, z in ((0, S - 1), (1, 0)):
            plane = us[pl.ds(z, PL, stride=S), :]
            packed = jnp.where(low_half, plane[: PL // 2], plane[PL // 2 :])
            halo_out[field, way] = packed.astype(BF16)
            halo_copy(field, way).start()

    def receive_halo(field):
        for way in range(2):
            halo_copy(field, way).wait_recv()
            got = halo_in[field, way].astype(F32)
            exists = (b > 0) if way == 0 else (b < nb - 1)
            got = got * jnp.where(exists, 1.0, 0.0)
            swapped = pltpu.roll(got, C, 1)
            halo_wide[way, : PL // 2, :] = jnp.where(low_half, got, swapped)
            halo_wide[way, PL // 2 :, :] = jnp.where(low_half, swapped, got)

    low_plane = low_lanes(PL)
    z_of = lax.broadcasted_iota(jnp.int32, (PL, L), 0) & (S - 1)

    def rows_of(x):
        return slice(x * PL, x * PL + PL)

    def fill(field):
        for x in range(S):
            u = us[rows_of(x), :]
            at = slice(x * S, x * S + S)
            low_z = jnp.broadcast_to(halo_wide[0, at, :][:, None, :], (S, S, L)).reshape(PL, L)
            high_z = jnp.broadcast_to(halo_wide[1, at, :][:, None, :], (S, S, L)).reshape(PL, L)
            down = jnp.where(z_of == 0, low_z, pltpu.roll(u, 1, 0))
            up = jnp.where(z_of == S - 1, high_z, pltpu.roll(u, PL - 1, 0))
            tile = jnp.where(low_plane, down, u)
            field[x, 1 : S + 1, :, :L] = tile.reshape(S, S, L).astype(BF16)
            field[x, 1 : S + 1, :, L:] = up.reshape(S, S, L).astype(BF16)

    def conv(field, number):
        rows = jnp.concatenate([field[:, e : e + S].reshape(S * PL, PL) for e in range(3)], axis=1)
        yy[1 : S + 1] = dot_nn(rows, wa[number]).reshape(S, PL, PL)

    def conv_result(x):
        sides = jnp.where(low_plane, yy[x, :, :L], yy[x + 2, :, :L])
        return sides + pltpu.roll(sides, C, 1) + yy[x + 1, :, L:]

    def turn(x, value):
        gt[(x + 1) * C : (x + 2) * C, :] = dot_nt(eye64w, value).astype(BF16)

    def weight_grad(field, number):
        left = jnp.concatenate([gt[x * C : (x + 3) * C, :] for x in range(S)], axis=1)
        for e in range(3):
            grads[e] = dot_nn(left, field[:, e : e + S].reshape(S * PL, PL))
        low = low_lanes(96)
        for e in range(3):
            for j in range(3):
                row = e * 3 * C + j * C
                pack[number, row // HALF, row % HALF : row % HALF + C, :] = grads[e, j * C : j * C + C, :L]
            row = 9 * C + e * 96 - HALF
            pack[number, 1, row : row + 96, :] = jnp.where(low, grads[e, :96, L:], grads[e, 96:, L:])

    def pack_bias(number, total):
        row = jnp.sum(total, axis=0, keepdims=True)
        pack[number, 1, BIAS_ROW : BIAS_ROW + 1, :] = row

    chunk = HALF // nq

    def split_bias(value, first_row):
        row = lax.broadcasted_iota(jnp.int32, value.shape, 0) + first_row
        at = BIAS_ROW % chunk if value.shape[0] == chunk else BIAS_ROW
        whole = value[at : at + 1] + value[at + 1 : at + 2]
        high = whole.astype(BF16).astype(F32)
        value = jnp.where(row == HALF + BIAS_ROW, high, value)
        return jnp.where(row == HALF + BIAS_ROW + 1, whole - high, value)

    def pair_copy(number, step):
        if step == 0:
            src, dst = pack.at[number, 1 - core], part1.at[number]
        else:
            src, dst = full.at[number, core], full.at[number, core]
        return copy_to(src, dst, pair_send.at[number, step], pair_recv.at[number, step], {"bricks": other})

    def reduce_chips_copy(number, j):
        return copy_to(
            sum1.at[number, lax.rem(q + j, nq)],
            part2.at[number, j],
            chip_send.at[number, 0, j],
            chip_recv.at[number, 0, j],
            chip_at(j),
        )

    def scene_copy(number, j, sender):
        return copy_to(
            sum2.at[number],
            part3.at[number, sender],
            scene_send.at[number, j],
            scene_recv.at[number, j],
            scene_at(j),
        )

    def gather_chips_copy(number, j, sender):
        return copy_to(
            sum3.at[number],
            full.at[number, core, sender],
            chip_send.at[number, 1, j],
            chip_recv.at[number, 1, j],
            chip_at(j),
        )

    def sum_start(number):
        pair_copy(number, 0).start()

    def sum_chips(number):
        pair_copy(number, 0).wait_recv()
        total = split_bias(pack[number, core] + part1[number], core * HALF)
        sum1[number] = total.astype(BF16).reshape(nq, chunk, L)
        for j in range(1, nq):
            reduce_chips_copy(number, j).start()

    def sum_scenes(number):
        for j in range(1, nq):
            reduce_chips_copy(number, j).wait_recv()
        total = sum1[number, q].astype(F32)
        for j in range(1, nq):
            total += part2[number, j].astype(F32)
        total = split_bias(total, core * HALF + q * chunk).astype(BF16)
        sum2[number] = total
        part3[number, s] = total
        for j in range(1, ns):
            scene_copy(number, j, s).start()

    def gather_chips(number):
        for j in range(1, ns):
            scene_copy(number, j, lax.rem(s + ns - j, ns)).wait_recv()
        total = part3[number, 0].astype(F32)
        for j in range(1, ns):
            total += part3[number, j].astype(F32)
        total = split_bias(total, core * HALF + q * chunk).astype(BF16)
        sum3[number] = total
        full[number, core, q] = total
        for j in range(1, nq):
            gather_chips_copy(number, j, q).start()

    def gather_pair(number):
        for j in range(1, nq):
            gather_chips_copy(number, j, lax.rem(q + nq - j, nq)).wait_recv()
        pair_copy(number, 1).start()

    def sum_end(number):
        pair_copy(number, 1).wait_recv()

    def sends_end(number):
        pair_copy(number, 0).wait_send()
        pair_copy(number, 1).wait_send()
        for j in range(1, nq):
            reduce_chips_copy(number, j).wait_send()
            gather_chips_copy(number, j, q).wait_send()
        for j in range(1, ns):
            scene_copy(number, j, s).wait_send()

    for field in (f0, f1, f2):
        field[:, 0] = jnp.zeros((S, S, PL), BF16)
        field[:, S + 1] = jnp.zeros((S, S, PL), BF16)
    yy[0] = jnp.zeros((PL, PL), F32)
    yy[S + 1] = jnp.zeros((PL, PL), F32)
    gt[:C] = jnp.zeros((C, PL), BF16)
    gt[(S + 1) * C :] = jnp.zeros((C, PL), BF16)
    for number in range(2):
        pack[number, 1, BIAS_ROW:, :] = jnp.zeros((HALF - BIAS_ROW, L), F32)

    for column in range(4):
        load_features(column)
    for x in range(S):
        us[rows_of(x), :] = u0[x].reshape(PL, L)
    pl.semaphore_wait(barrier, 2 + (nq - 1) + (ns - 1))
    send_halo(0)
    prepare_weights(w1, 0, True)
    receive_halo(0)
    fill(f0)
    conv(f0, 0)

    def after_first(x):
        live = mm[x].reshape(PL, L)
        bias = jnp.concatenate([b1[...], b1[...]], axis=1)
        first = live * (conv_result(x) + bias)
        sig = sigmoid(first)
        hidden = first * sig
        sl[rows_of(x), :] = live * (sig + hidden * (1.0 - sig))
        us[rows_of(x), :] = hidden.astype(BF16).astype(F32)

    for x in range(S):
        after_first(x)
    send_halo(1)
    w2_load.wait()
    prepare_weights(w2, 1, True)
    prepare_weights(w2, 2, False)
    prepare_weights(w1, 3, False)
    cot_load.wait()
    for column in range(4):
        load_cotangent(column)
    receive_halo(1)
    fill(f1)
    conv(f1, 1)

    def after_second(x):
        live = mm[x].reshape(PL, L)
        bias = jnp.concatenate([b2[...], b2[...]], axis=1)
        summed = live * (conv_result(x) + bias) + u0[x].reshape(PL, L)
        sig = sigmoid(summed)
        value = summed * sig
        oo[x] = value.reshape(S, S, L)
        slope = sig + value * (1.0 - sig)
        grad = (ct[x].reshape(PL, L) * slope * live).astype(BF16)
        turn(x, grad)
        grad = grad.astype(F32)
        us[rows_of(x), :] = grad
        gs[rows_of(x), :] = grad
        return jnp.sum(grad.reshape(PL // 8, 8, L), axis=0)

    total = jnp.zeros((8, L), F32)
    for x in range(S):
        total += after_second(x)
    send_halo(2)
    pack_bias(1, total)
    weight_grad(f1, 1)
    sum_start(1)
    receive_halo(2)
    fill(f2)
    conv(f2, 2)
    sum_chips(1)

    def after_third(x):
        grad = (conv_result(x) * sl[rows_of(x), :]).astype(BF16)
        turn(x, grad)
        grad = grad.astype(F32)
        us[rows_of(x), :] = grad
        return jnp.sum(grad.reshape(PL // 8, 8, L), axis=0)

    total = jnp.zeros((8, L), F32)
    for x in range(S):
        total += after_third(x)
    send_halo(3)
    pack_bias(0, total)
    weight_grad(f0, 0)
    sum_start(0)
    sum_scenes(1)
    sum_chips(0)
    receive_halo(3)
    fill(f2)
    conv(f2, 3)

    def after_fourth(x):
        value = mm[x].reshape(PL, L) * (gs[rows_of(x), :] + conv_result(x))
        o2[x] = value.reshape(S, S, L)

    gather_chips(1)
    store_bricks(oo, out)
    sum_scenes(0)
    for x in range(S):
        after_fourth(x)
    gather_pair(1)
    gather_chips(0)
    store_bricks(o2, gfeat)
    sum_end(1)
    sums[1] = full[1].reshape(2, HALF, L)
    gather_pair(0)
    sends_end(1)
    sum_end(0)
    sums[0] = full[0].reshape(2, HALF, L)
    sends_end(0)
    for field in range(4):
        for way in range(2):
            halo_copy(field, way).wait_send()


def unpack(sums, number, weight, bias):
    low = low_lanes(C)

    def packed(row, size):
        return sums[number, row // HALF, row % HALF : row % HALF + size, :].astype(F32)

    def piece(k):
        dx, dy, dz = k // 9, k // 3 % 3, k % 3
        j = 2 - dx
        if dz < 2:
            return packed(dy * 3 * C + j * C, C), dz
        base = 9 * C + dy * 96
        if j == 0:
            return packed(base, C), 0
        if j == 2:
            return packed(base + 32, C), 1
        first = packed(base + 64, 32)
        second = pltpu.roll(packed(base, 32), C, 1)
        return jnp.concatenate([first, second], axis=0), 0

    def placed(k, half):
        value, at = piece(k)
        return value if at == half else pltpu.roll(value, C, 1)

    for m in range(13):
        weight[:, m * L : m * L + L] = jnp.where(low, placed(2 * m, 0), placed(2 * m + 1, 1))
    weight[:, 13 * L :] = placed(26, 0)[:, :C]
    rows = packed(HALF + BIAS_ROW, 16)
    bias[...] = (rows[0:1] + rows[1:2])[:, :C]


def finish(out_in, gfeat_in, sums, out, gfeat, gw1, gw2, gb1, gb2):
    out[...] = out_in[...]
    gfeat[...] = gfeat_in[...]
    unpack(sums, 0, gw1, gb1)
    unpack(sums, 1, gw2, gb2)


def local(nb, ns, features, cotangent, mask, w1, b1, w2, b2):
    nq = nb // 2
    chunk = HALF // nq
    vmem = pltpu.VMEM
    field = vmem((S, S + 2, S, PL), BF16)
    block4 = vmem((S, S, S, L), F32)
    block2 = vmem((S * PL, L), F32)
    dma = pltpu.SemaphoreType.DMA
    scratch = [
        vmem(features.shape, BF16),
        vmem(w2.shape, BF16),
        field,
        field,
        field,
        vmem((S + 2, PL, PL), F32),
        vmem(((S + 2) * C, PL), BF16),
        block4,
        block4,
        block4,
        block2,
        block2,
        block2,
        block4,
        block4,
        vmem((27 * C, L), F32),
        vmem((27 * C, L), F32),
        vmem((4, 3 * PL, PL), BF16),
        vmem((4, 2, PL // 2, L), BF16),
        vmem((4, 2, PL // 2, L), BF16),
        vmem((2, PL, L), F32),
        vmem((3, 3 * C, PL), F32),
        vmem((2, 2, HALF, L), F32),
        vmem((2, HALF, L), F32),
        vmem((2, nq, chunk, L), BF16),
        vmem((2, nq, chunk, L), BF16),
        vmem((2, chunk, L), BF16),
        vmem((2, ns, chunk, L), BF16),
        vmem((2, chunk, L), BF16),
        vmem((2, 2, nq, chunk, L), BF16),
        dma((4, 2)),
        dma((4, 2)),
        dma((2, 2)),
        dma((2, 2)),
        dma((2, 2, nq)),
        dma((2, 2, nq)),
        dma((2, ns)),
        dma((2, ns)),
        dma((2,)),
    ]
    shape = jax.ShapeDtypeStruct
    in_vmem = pl.BlockSpec(memory_space=pltpu.VMEM)
    anywhere = pl.BlockSpec(memory_space=pl.ANY)
    output, grad_features, sums = pl.pallas_call(
        functools.partial(kernel, nb, ns),
        out_shape=[
            shape(features.shape, BF16),
            shape(features.shape, BF16),
            shape((2, 2, HALF, L), BF16),
        ],
        in_specs=[in_vmem, anywhere, in_vmem, in_vmem, in_vmem, anywhere, in_vmem],
        out_specs=[in_vmem] * 3,
        scratch_shapes=scratch,
        compiler_params=pltpu.CompilerParams(
            collective_id=0, has_side_effects=True, vmem_limit_bytes=56 * 1024 * 1024
        ),
        name="residual_block",
    )(features, cotangent, mask, w1, b1.reshape(1, C), w2, b2.reshape(1, C))
    output, grad_features, gw1, gw2, gb1, gb2 = pl.pallas_call(
        finish,
        out_shape=[
            shape(features.shape, BF16),
            shape(features.shape, BF16),
            shape(w1.shape, F32),
            shape(w2.shape, F32),
            shape((1, C), F32),
            shape((1, C), F32),
        ],
        in_specs=[in_vmem] * 3,
        out_specs=[in_vmem] * 6,
        name="finish",
    )(output, grad_features, sums)
    return output, grad_features, gw1, gw2, gb1.reshape(C), gb2.reshape(C)


def solution(mesh):
    nb, ns = mesh.shape["bricks"], mesh.shape["scenes"]

    def program(features, cotangent, neighbours, mask, weight_one, bias_one, weight_two, bias_two):
        del neighbours
        split = P("scenes", "bricks", None, None)
        return jax.shard_map(
            functools.partial(local, nb, ns),
            mesh=mesh,
            in_specs=(split, split, P("scenes", "bricks", None), P(), P(), P(), P()),
            out_specs=(split, split, P(), P(), P(), P()),
            check_vma=False,
        )(features, cotangent, mask, weight_one, bias_one, weight_two, bias_two)

    return program
```

```python
import functools

import jax
import jax.numpy as jnp
from jax import lax
from jax.experimental import pallas as pl
from jax.experimental.pallas import tpu as pltpu
from jax.sharding import PartitionSpec as P

C = 64
E = 8
S = 16
PL = S * S
L = 128
HALF = 512
BIAS_ROW = 864 - HALF
F32 = jnp.float32
BF16 = jnp.bfloat16


def dot_nn(a, b):
    return lax.dot_general(a, b, (((1,), (0,)), ((), ())), preferred_element_type=F32)


def dot_nt(a, b):
    return lax.dot_general(a, b, (((1,), (1,)), ((), ())), preferred_element_type=F32)


def eye(rows, cols):
    r = lax.broadcasted_iota(jnp.int32, (rows, cols), 0)
    c = lax.broadcasted_iota(jnp.int32, (rows, cols), 1)
    return jnp.where(r == c, 1.0, 0.0).astype(BF16)


def low_lanes(rows):
    return lax.broadcasted_iota(jnp.int32, (rows, L), 1) < C


def tap_of(dx, dy, dz):
    return 9 * (dx + 1) + 3 * (dy + 1) + (dz + 1)


def copy_to(src, dst, send, recv, device):
    return pltpu.make_async_remote_copy(
        src_ref=src,
        dst_ref=dst,
        send_sem=send,
        recv_sem=recv,
        device_id=device,
        device_id_type=pl.DeviceIdType.MESH,
    )


def sigmoid(v):
    return 1.0 / (1.0 + jnp.exp(-v))


def kernel(
    nb,
    ns,
    feat,
    cot_hbm,
    mask,
    w1,
    b1,
    w2_hbm,
    b2,
    out,
    gfeat,
    sums,
    cot,
    w2,
    f0,
    f1,
    f2,
    yy,
    gt,
    u0,
    mm,
    ct,
    us,
    sl,
    gs,
    oo,
    o2,
    wt,
    wd,
    wa,
    halo_out,
    halo_in,
    halo_wide,
    added,
    grads,
    pack,
    part1,
    sum1,
    part2,
    sum2,
    part3,
    sum3,
    full,
    halo_send,
    halo_recv,
    pair_send,
    pair_recv,
    chip_send,
    chip_recv,
    scene_send,
    scene_recv,
    load_sem,
):
    nq = nb // 2
    b = lax.axis_index("bricks")
    s = lax.axis_index("scenes")
    core = lax.rem(b, 2)
    q = b // 2
    below = lax.rem(b + nb - 1, nb)
    above = lax.rem(b + 1, nb)
    other = b + 1 - 2 * core

    nx = 4 if nq % 4 == 0 else nq
    ny = nq // nx
    cx, cy = lax.rem(q, nx), q // nx

    def far(step, size):
        return min(step, size - step)

    chip_steps = [(dy, dx) for dy in range(ny) for dx in range(nx)][1:]
    chip_steps = [None] + sorted(chip_steps, key=lambda t: -far(t[0], ny) - far(t[1], nx))
    scene_steps = [None] + sorted(range(1, ns), key=lambda t: -far(t, ns))

    def chip_to(j):
        dy, dx = chip_steps[j]
        return lax.rem(cy + dy, ny) * nx + lax.rem(cx + dx, nx)

    def chip_from(j):
        dy, dx = chip_steps[j]
        return lax.rem(cy + ny - dy, ny) * nx + lax.rem(cx + nx - dx, nx)

    def chip_at(j):
        return {"bricks": 2 * chip_to(j) + core}

    def scene_at(j):
        return {"scenes": lax.rem(s + scene_steps[j], ns)}

    def scene_from(j):
        return lax.rem(s + ns - scene_steps[j], ns)

    cot_load = pltpu.make_async_copy(cot_hbm, cot, load_sem.at[0])
    w2_load = pltpu.make_async_copy(w2_hbm, w2, load_sem.at[1])
    cot_load.start()
    w2_load.start()

    barrier = pltpu.get_barrier_semaphore()

    def greet(device):
        pl.semaphore_signal(barrier, inc=1, device_id=device, device_id_type=pl.DeviceIdType.MESH)

    greet({"bricks": below})
    greet({"bricks": above})
    for j in range(1, nq):
        greet(chip_at(j))
    for j in range(1, ns):
        greet(scene_at(j))

    eye256 = eye(PL, PL)
    eye128 = eye(L, L)
    eye64 = eye(C, C)
    eye64w = eye(C, L)

    def load_features(column):
        bx, by = column // 2, column % 2
        for bz in range(2):
            n = column * 2 + bz
            live = mask[0, n : n + 1, :].astype(F32)
            live = jnp.broadcast_to(live, (L, 2 * PL)).astype(BF16)
            masked = feat[0, n] * live[:C]
            for h in range(2):
                cols = slice(h * PL, (h + 1) * PL)
                stack = jnp.concatenate([masked[:, cols], masked[:, cols], live[:, cols]], axis=0)
                turned = dot_nt(eye256, stack)
                x, y, z = bx * E + 4 * h, by * E, bz * E
                place = (slice(x, x + 4), slice(y, y + E), slice(z, z + E))
                u0[place] = turned[:, :L].reshape(4, E, E, L)
                mm[place] = turned[:, L:].reshape(4, E, E, L)

    def load_cotangent(column):
        bx, by = column // 2, column % 2
        for bz in range(2):
            value = cot[0, column * 2 + bz]
            for h in range(2):
                cols = slice(h * PL, (h + 1) * PL)
                stack = jnp.concatenate([value[:, cols], value[:, cols]], axis=0)
                x, y, z = bx * E + 4 * h, by * E, bz * E
                place = (slice(x, x + 4), slice(y, y + E), slice(z, z + E))
                ct[place] = dot_nt(eye256, stack).reshape(4, E, E, L)

    def store_bricks(oo, target):
        for n in range(8):
            bx, by, bz = n // 4, n // 2 % 2, n % 2
            rows = oo[bx * E : bx * E + E, by * E : by * E + E, bz * E : bz * E + E, :]
            rows = rows.reshape(E * E * E, L).astype(BF16)
            target[0, n] = dot_nt(eye64w, rows).astype(BF16)

    def prepare_weights(w, number, forward):
        spread = jnp.concatenate([eye64, eye64], axis=1)
        for m in range(14):
            size = L if m < 13 else C
            tile = w[:, m * L : m * L + size]
            if forward:
                twice = jnp.concatenate([tile, tile], axis=0)
                wt[m * L : m * L + size, :] = dot_nt(eye128 if m < 13 else eye64, twice)
            else:
                for part in range(size // C):
                    zeros = jnp.zeros((C, L), BF16)
                    if m == 13:
                        select = spread
                    else:
                        select = jnp.concatenate([spread, zeros] if part == 0 else [zeros, spread], axis=0)
                    k = 2 * m + part
                    wd[k * C : k * C + C, :] = dot_nn(tile, select)
        low = low_lanes(C)
        for dy in (-1, 0, 1):
            for i, dz in enumerate((-1, 0, 1)):

                def block(dx):
                    if forward:
                        k = tap_of(dx, dy, dz)
                        return wt[k * C : k * C + C, :]
                    k = tap_of(-dx, -dy, -dz)
                    return wd[k * C : k * C + C, :]

                rows = slice((dy + 1) * PL + i * C, (dy + 1) * PL + i * C + C)
                wa[number, rows, :L] = jnp.where(low, block(-1), block(1)).astype(BF16)
                wa[number, rows, L:] = block(0).astype(BF16)
            wa[number, (dy + 1) * PL + 3 * C : (dy + 2) * PL, :] = jnp.zeros((C, PL), BF16)

    low_half = low_lanes(PL // 2)

    def halo_copy(field, way):
        return copy_to(
            halo_out.at[field, way],
            halo_in.at[field, way],
            halo_send.at[field, way],
            halo_recv.at[field, way],
            {"bricks": above if way == 0 else below},
        )

    def send_halo(field):
        for way, z in ((0, S - 1), (1, 0)):
            plane = us[pl.ds(z, PL, stride=S), :]
            packed = jnp.where(low_half, plane[: PL // 2], plane[PL // 2 :])
            halo_out[field, way] = packed.astype(BF16)
            halo_copy(field, way).start()

    def receive_halo(field):
        for way in range(2):
            halo_copy(field, way).wait_recv()
            got = halo_in[field, way].astype(F32)
            exists = (b > 0) if way == 0 else (b < nb - 1)
            got = got * jnp.where(exists, 1.0, 0.0)
            swapped = pltpu.roll(got, C, 1)
            halo_wide[field, way, : PL // 2, :] = jnp.where(low_half, got, swapped)
            halo_wide[field, way, PL // 2 :, :] = jnp.where(low_half, swapped, got)

    def add_halo(field, number):
        for way in range(2):
            plane = halo_wide[field, way]
            down = jnp.where(z_of == 0, 0.0, pltpu.roll(plane, 1, 0))
            up = jnp.where(z_of == S - 1, 0.0, pltpu.roll(plane, PL - 1, 0))
            rows = jnp.concatenate([jnp.where(low_plane, down, plane), up], axis=1).astype(BF16)
            taps = [wa[number, e * PL + 2 * C * way : e * PL + 2 * C * way + C, :] for e in range(3)]
            taps = jnp.concatenate(taps + [jnp.zeros((C, PL), BF16)], axis=0)
            got = dot_nn(rows, taps)
            edge = jnp.zeros((S, L), F32)
            left = jnp.concatenate([edge, got[: PL - S, :L]], axis=0)
            right = jnp.concatenate([got[S:, :L], edge], axis=0)
            sides = jnp.where(low_plane, left, right)
            added[way] = sides + pltpu.roll(sides, C, 1) + got[:, L:]

    low_plane = low_lanes(PL)
    z_of = lax.broadcasted_iota(jnp.int32, (PL, L), 0) & (S - 1)

    def rows_of(x):
        return slice(x * PL, x * PL + PL)

    def spread(ref, x):
        rows = ref[x * S : x * S + S, :]
        return jnp.broadcast_to(rows[:, None, :], (S, S, L)).reshape(PL, L)

    def fill(field, x, u):
        down = jnp.where(z_of == 0, 0.0, pltpu.roll(u, 1, 0))
        up = jnp.where(z_of == S - 1, 0.0, pltpu.roll(u, PL - 1, 0))
        tile = jnp.where(low_plane, down, u)
        field[x, 1 : S + 1, :, :L] = tile.reshape(S, S, L).astype(BF16)
        field[x, 1 : S + 1, :, L:] = up.reshape(S, S, L).astype(BF16)

    def fill_halo(field, number):
        below_at = (z_of == 0) & low_plane
        above_at = z_of == S - 1
        for x in range(S):
            tile = field[x, 1 : S + 1, :, :L].reshape(PL, L).astype(F32)
            tile = jnp.where(below_at, spread(halo_wide.at[number, 0], x), tile)
            field[x, 1 : S + 1, :, :L] = tile.reshape(S, S, L).astype(BF16)
            tile = field[x, 1 : S + 1, :, L:].reshape(PL, L).astype(F32)
            tile = jnp.where(above_at, spread(halo_wide.at[number, 1], x), tile)
            field[x, 1 : S + 1, :, L:] = tile.reshape(S, S, L).astype(BF16)

    def conv(field, number):
        rows = jnp.concatenate([field[:, e : e + S].reshape(S * PL, PL) for e in range(3)], axis=1)
        yy[1 : S + 1] = dot_nn(rows, wa[number]).reshape(S, PL, PL)

    def conv_result(x):
        sides = jnp.where(low_plane, yy[x, :, :L], yy[x + 2, :, :L])
        outer = jnp.where(z_of == 0, spread(added.at[0], x), spread(added.at[1], x))
        outer = jnp.where((z_of == 0) | (z_of == S - 1), outer, 0.0)
        return sides + pltpu.roll(sides, C, 1) + yy[x + 1, :, L:] + outer

    def turn(x, value):
        gt[(x + 1) * C : (x + 2) * C, :] = dot_nt(eye64w, value).astype(BF16)

    def weight_grad(field, number):
        left = jnp.concatenate([gt[x * C : (x + 3) * C, :] for x in range(S)], axis=1)
        for e in range(3):
            grads[e] = dot_nn(left, field[:, e : e + S].reshape(S * PL, PL))
        low = low_lanes(96)
        for e in range(3):
            for j in range(3):
                row = e * 3 * C + j * C
                pack[number, row // HALF, row % HALF : row % HALF + C, :] = grads[e, j * C : j * C + C, :L]
            row = 9 * C + e * 96 - HALF
            pack[number, 1, row : row + 96, :] = jnp.where(low, grads[e, :96, L:], grads[e, 96:, L:])

    def pack_bias(number, total):
        row = jnp.sum(total, axis=0, keepdims=True)
        pack[number, 1, BIAS_ROW : BIAS_ROW + 1, :] = row

    chunk = HALF // nq

    def split_bias(value, first_row):
        row = lax.broadcasted_iota(jnp.int32, value.shape, 0) + first_row
        at = BIAS_ROW % chunk if value.shape[0] == chunk else BIAS_ROW
        whole = value[at : at + 1] + value[at + 1 : at + 2]
        high = whole.astype(BF16).astype(F32)
        value = jnp.where(row == HALF + BIAS_ROW, high, value)
        return jnp.where(row == HALF + BIAS_ROW + 1, whole - high, value)

    def pair_copy(number, step):
        if step == 0:
            src, dst = pack.at[number, 1 - core], part1.at[number]
        else:
            src, dst = full.at[number, core], full.at[number, core]
        return copy_to(src, dst, pair_send.at[number, step], pair_recv.at[number, step], {"bricks": other})

    def reduce_chips_copy(number, j):
        return copy_to(
            sum1.at[number, chip_to(j)],
            part2.at[number, j],
            chip_send.at[number, 0, j],
            chip_recv.at[number, 0, j],
            chip_at(j),
        )

    def scene_copy(number, j, sender):
        return copy_to(
            sum2.at[number],
            part3.at[number, sender],
            scene_send.at[number, j],
            scene_recv.at[number, j],
            scene_at(j),
        )

    def gather_chips_copy(number, j, sender):
        return copy_to(
            sum3.at[number],
            full.at[number, core, sender],
            chip_send.at[number, 1, j],
            chip_recv.at[number, 1, j],
            chip_at(j),
        )

    def sum_start(number):
        pair_copy(number, 0).start()

    def sum_chips(number):
        pair_copy(number, 0).wait_recv()
        total = split_bias(pack[number, core] + part1[number], core * HALF)
        sum1[number] = total.astype(BF16).reshape(nq, chunk, L)
        for j in range(1, nq):
            reduce_chips_copy(number, j).start()

    def sum_scenes(number):
        for j in range(1, nq):
            reduce_chips_copy(number, j).wait_recv()
        total = sum1[number, q].astype(F32)
        for j in range(1, nq):
            total += part2[number, j].astype(F32)
        total = split_bias(total, core * HALF + q * chunk).astype(BF16)
        sum2[number] = total
        part3[number, s] = total
        for j in range(1, ns):
            scene_copy(number, j, s).start()

    def gather_chips(number):
        for j in range(1, ns):
            scene_copy(number, j, scene_from(j)).wait_recv()
        total = part3[number, 0].astype(F32)
        for j in range(1, ns):
            total += part3[number, j].astype(F32)
        total = split_bias(total, core * HALF + q * chunk).astype(BF16)
        sum3[number] = total
        full[number, core, q] = total
        for j in range(1, nq):
            gather_chips_copy(number, j, q).start()

    def gather_pair(number):
        for j in range(1, nq):
            gather_chips_copy(number, j, chip_from(j)).wait_recv()
        pair_copy(number, 1).start()

    def sum_end(number):
        pair_copy(number, 1).wait_recv()

    def sends_end(number):
        pair_copy(number, 0).wait_send()
        pair_copy(number, 1).wait_send()
        for j in range(1, nq):
            reduce_chips_copy(number, j).wait_send()
            gather_chips_copy(number, j, q).wait_send()
        for j in range(1, ns):
            scene_copy(number, j, s).wait_send()

    for field in (f0, f1, f2):
        field[:, 0] = jnp.zeros((S, S, PL), BF16)
        field[:, S + 1] = jnp.zeros((S, S, PL), BF16)
    yy[0] = jnp.zeros((PL, PL), F32)
    yy[S + 1] = jnp.zeros((PL, PL), F32)
    gt[:C] = jnp.zeros((C, PL), BF16)
    gt[(S + 1) * C :] = jnp.zeros((C, PL), BF16)
    for number in range(2):
        pack[number, 1, BIAS_ROW:, :] = jnp.zeros((HALF - BIAS_ROW, L), F32)

    for column in range(4):
        load_features(column)
    for x in range(S):
        us[rows_of(x), :] = u0[x].reshape(PL, L)
        fill(f0, x, u0[x].reshape(PL, L))
    pl.semaphore_wait(barrier, 2 + (nq - 1) + (ns - 1))
    send_halo(0)
    prepare_weights(w1, 0, True)
    conv(f0, 0)
    w2_load.wait()
    prepare_weights(w2, 1, True)
    prepare_weights(w2, 2, False)
    prepare_weights(w1, 3, False)
    cot_load.wait()
    for column in range(4):
        load_cotangent(column)
    receive_halo(0)
    add_halo(0, 0)

    def after_first(x):
        live = mm[x].reshape(PL, L)
        bias = jnp.concatenate([b1[...], b1[...]], axis=1)
        first = live * (conv_result(x) + bias)
        sig = sigmoid(first)
        hidden = first * sig
        sl[rows_of(x), :] = live * (sig + hidden * (1.0 - sig))
        hidden = hidden.astype(BF16).astype(F32)
        us[rows_of(x), :] = hidden
        fill(f1, x, hidden)

    for x in range(S):
        after_first(x)
    send_halo(1)
    conv(f1, 1)
    fill_halo(f0, 0)
    receive_halo(1)
    add_halo(1, 1)

    def after_second(x):
        live = mm[x].reshape(PL, L)
        bias = jnp.concatenate([b2[...], b2[...]], axis=1)
        summed = live * (conv_result(x) + bias) + u0[x].reshape(PL, L)
        sig = sigmoid(summed)
        value = summed * sig
        oo[x] = value.reshape(S, S, L)
        slope = sig + value * (1.0 - sig)
        grad = (ct[x].reshape(PL, L) * slope * live).astype(BF16)
        turn(x, grad)
        grad = grad.astype(F32)
        us[rows_of(x), :] = grad
        gs[rows_of(x), :] = grad
        fill(f2, x, grad)
        return jnp.sum(grad.reshape(PL // 8, 8, L), axis=0)

    total = jnp.zeros((8, L), F32)
    for x in range(S):
        total += after_second(x)
    send_halo(2)
    pack_bias(1, total)
    conv(f2, 2)
    fill_halo(f1, 1)
    weight_grad(f1, 1)
    sum_start(1)
    receive_halo(2)
    add_halo(2, 2)

    def after_third(x):
        grad = (conv_result(x) * sl[rows_of(x), :]).astype(BF16)
        turn(x, grad)
        grad = grad.astype(F32)
        us[rows_of(x), :] = grad
        fill(f2, x, grad)
        return jnp.sum(grad.reshape(PL // 8, 8, L), axis=0)

    total = jnp.zeros((8, L), F32)
    for x in range(S):
        total += after_third(x)
    send_halo(3)
    pack_bias(0, total)
    sum_chips(1)
    weight_grad(f0, 0)
    sum_start(0)
    conv(f2, 3)
    sum_chips(0)
    sum_scenes(1)
    receive_halo(3)
    add_halo(3, 3)

    def after_fourth(x):
        value = mm[x].reshape(PL, L) * (gs[rows_of(x), :] + conv_result(x))
        o2[x] = value.reshape(S, S, L)

    store_bricks(oo, out)
    for x in range(S):
        after_fourth(x)
    sum_scenes(0)
    gather_chips(1)
    store_bricks(o2, gfeat)
    gather_chips(0)
    gather_pair(1)
    sum_end(1)
    sums[1] = full[1].reshape(2, HALF, L)
    gather_pair(0)
    sends_end(1)
    sum_end(0)
    sums[0] = full[0].reshape(2, HALF, L)
    sends_end(0)
    for field in range(4):
        for way in range(2):
            halo_copy(field, way).wait_send()


def unpack(sums, number, weight, bias):
    low = low_lanes(C)

    def packed(row, size):
        return sums[number, row // HALF, row % HALF : row % HALF + size, :].astype(F32)

    def piece(k):
        dx, dy, dz = k // 9, k // 3 % 3, k % 3
        j = 2 - dx
        if dz < 2:
            return packed(dy * 3 * C + j * C, C), dz
        base = 9 * C + dy * 96
        if j == 0:
            return packed(base, C), 0
        if j == 2:
            return packed(base + 32, C), 1
        first = packed(base + 64, 32)
        second = pltpu.roll(packed(base, 32), C, 1)
        return jnp.concatenate([first, second], axis=0), 0

    def placed(k, half):
        value, at = piece(k)
        return value if at == half else pltpu.roll(value, C, 1)

    for m in range(13):
        weight[:, m * L : m * L + L] = jnp.where(low, placed(2 * m, 0), placed(2 * m + 1, 1))
    weight[:, 13 * L :] = placed(26, 0)[:, :C]
    rows = packed(HALF + BIAS_ROW, 16)
    bias[...] = (rows[0:1] + rows[1:2])[:, :C]


def finish(out_in, gfeat_in, sums, out, gfeat, gw1, gw2, gb1, gb2, sem):
    copies = [
        pltpu.make_async_copy(out_in, out, sem.at[0]),
        pltpu.make_async_copy(gfeat_in, gfeat, sem.at[1]),
    ]
    for copy in copies:
        copy.start()
    unpack(sums, 0, gw1, gb1)
    unpack(sums, 1, gw2, gb2)
    for copy in copies:
        copy.wait()


def local(nb, ns, features, cotangent, mask, w1, b1, w2, b2):
    nq = nb // 2
    chunk = HALF // nq
    vmem = pltpu.VMEM
    field = vmem((S, S + 2, S, PL), BF16)
    block4 = vmem((S, S, S, L), F32)
    block2 = vmem((S * PL, L), F32)
    dma = pltpu.SemaphoreType.DMA
    scratch = [
        vmem(features.shape, BF16),
        vmem(w2.shape, BF16),
        field,
        field,
        field,
        vmem((S + 2, PL, PL), F32),
        vmem(((S + 2) * C, PL), BF16),
        block4,
        block4,
        block4,
        block2,
        block2,
        block2,
        block4,
        block4,
        vmem((27 * C, L), F32),
        vmem((27 * C, L), F32),
        vmem((4, 3 * PL, PL), BF16),
        vmem((4, 2, PL // 2, L), BF16),
        vmem((4, 2, PL // 2, L), BF16),
        vmem((4, 2, PL, L), F32),
        vmem((2, PL, L), F32),
        vmem((3, 3 * C, PL), F32),
        vmem((2, 2, HALF, L), F32),
        vmem((2, HALF, L), F32),
        vmem((2, nq, chunk, L), BF16),
        vmem((2, nq, chunk, L), BF16),
        vmem((2, chunk, L), BF16),
        vmem((2, ns, chunk, L), BF16),
        vmem((2, chunk, L), BF16),
        vmem((2, 2, nq, chunk, L), BF16),
        dma((4, 2)),
        dma((4, 2)),
        dma((2, 2)),
        dma((2, 2)),
        dma((2, 2, nq)),
        dma((2, 2, nq)),
        dma((2, ns)),
        dma((2, ns)),
        dma((2,)),
    ]
    shape = jax.ShapeDtypeStruct
    in_vmem = pl.BlockSpec(memory_space=pltpu.VMEM)
    anywhere = pl.BlockSpec(memory_space=pl.ANY)
    output, grad_features, sums = pl.pallas_call(
        functools.partial(kernel, nb, ns),
        out_shape=[
            pltpu.VMEM(features.shape, BF16),
            pltpu.VMEM(features.shape, BF16),
            pltpu.VMEM((2, 2, HALF, L), BF16),
        ],
        in_specs=[in_vmem, anywhere, in_vmem, in_vmem, in_vmem, anywhere, in_vmem],
        out_specs=[in_vmem] * 3,
        scratch_shapes=scratch,
        compiler_params=pltpu.CompilerParams(
            collective_id=0, has_side_effects=True, vmem_limit_bytes=56 * 1024 * 1024
        ),
        name="residual_block",
    )(features, cotangent, mask, w1, b1.reshape(1, C), w2, b2.reshape(1, C))
    output, grad_features, gw1, gw2, gb1, gb2 = pl.pallas_call(
        finish,
        out_shape=[
            shape(features.shape, BF16),
            shape(features.shape, BF16),
            shape(w1.shape, F32),
            shape(w2.shape, F32),
            shape((1, C), F32),
            shape((1, C), F32),
        ],
        in_specs=[in_vmem] * 3,
        out_specs=[anywhere] * 2 + [in_vmem] * 4,
        scratch_shapes=[dma((2,))],
        compiler_params=pltpu.CompilerParams(vmem_limit_bytes=8 * 1024 * 1024),
        name="finish",
    )(output, grad_features, sums)
    return output, grad_features, gw1, gw2, gb1.reshape(C), gb2.reshape(C)


def solution(mesh):
    nb, ns = mesh.shape["bricks"], mesh.shape["scenes"]

    def program(features, cotangent, neighbours, mask, weight_one, bias_one, weight_two, bias_two):
        del neighbours
        split = P("scenes", "bricks", None, None)
        return jax.shard_map(
            functools.partial(local, nb, ns),
            mesh=mesh,
            in_specs=(split, split, P("scenes", "bricks", None), P(), P(), P(), P()),
            out_specs=(split, split, P(), P(), P(), P()),
            check_vma=False,
        )(features, cotangent, mask, weight_one, bias_one, weight_two, bias_two)

    return program
```

```python
import functools

import jax
import jax.numpy as jnp
from jax import lax
from jax.experimental import pallas as pl
from jax.experimental.pallas import tpu as pltpu
from jax.sharding import PartitionSpec as P

C = 64
E = 8
S = 16
PL = S * S
L = 128
HALF = 512
BIAS_ROW = 864 - HALF
F32 = jnp.float32
BF16 = jnp.bfloat16


def dot_nn(a, b):
    return lax.dot_general(a, b, (((1,), (0,)), ((), ())), preferred_element_type=F32)


def dot_nt(a, b):
    return lax.dot_general(a, b, (((1,), (1,)), ((), ())), preferred_element_type=F32)


def eye(rows, cols):
    r = lax.broadcasted_iota(jnp.int32, (rows, cols), 0)
    c = lax.broadcasted_iota(jnp.int32, (rows, cols), 1)
    return jnp.where(r == c, 1.0, 0.0).astype(BF16)


def low_lanes(rows):
    return lax.broadcasted_iota(jnp.int32, (rows, L), 1) < C


def tap_of(dx, dy, dz):
    return 9 * (dx + 1) + 3 * (dy + 1) + (dz + 1)


def copy_to(src, dst, send, recv, device):
    return pltpu.make_async_remote_copy(
        src_ref=src,
        dst_ref=dst,
        send_sem=send,
        recv_sem=recv,
        device_id=device,
        device_id_type=pl.DeviceIdType.MESH,
    )


def sigmoid(v):
    return 1.0 / (1.0 + jnp.exp(-v))


def kernel(
    nb,
    ns,
    feat,
    cot_hbm,
    mask,
    w1,
    b1,
    w2_hbm,
    b2,
    out,
    gfeat,
    sums,
    cot,
    w2,
    f0,
    f1,
    f2,
    yy,
    gt,
    u0,
    mm,
    ct,
    us,
    sl,
    gs,
    oo,
    o2,
    wt,
    wd,
    wa,
    halo_out,
    halo_in,
    halo_wide,
    added,
    grads,
    pack,
    part1,
    sum1,
    part2,
    sum2,
    part3,
    sum3,
    full,
    halo_send,
    halo_recv,
    pair_send,
    pair_recv,
    chip_send,
    chip_recv,
    scene_send,
    scene_recv,
    load_sem,
):
    nq = nb // 2
    b = lax.axis_index("bricks")
    s = lax.axis_index("scenes")
    core = lax.rem(b, 2)
    q = b // 2
    below = lax.rem(b + nb - 1, nb)
    above = lax.rem(b + 1, nb)
    other = b + 1 - 2 * core

    nx = 4 if nq % 4 == 0 else nq
    ny = nq // nx
    cx, cy = lax.rem(q, nx), q // nx

    def far(step, size):
        return min(step, size - step)

    chip_steps = [(dy, dx) for dy in range(ny) for dx in range(nx)][1:]
    chip_steps = [None] + sorted(chip_steps, key=lambda t: -far(t[0], ny) - far(t[1], nx))
    scene_steps = [None] + sorted(range(1, ns), key=lambda t: -far(t, ns))

    def chip_to(j):
        dy, dx = chip_steps[j]
        return lax.rem(cy + dy, ny) * nx + lax.rem(cx + dx, nx)

    def chip_from(j):
        dy, dx = chip_steps[j]
        return lax.rem(cy + ny - dy, ny) * nx + lax.rem(cx + nx - dx, nx)

    def chip_at(j):
        return {"bricks": 2 * chip_to(j) + core}

    def scene_at(j):
        return {"scenes": lax.rem(s + scene_steps[j], ns)}

    def scene_from(j):
        return lax.rem(s + ns - scene_steps[j], ns)

    cot_load = pltpu.make_async_copy(cot_hbm, cot, load_sem.at[0])
    w2_load = pltpu.make_async_copy(w2_hbm, w2, load_sem.at[1])
    cot_load.start()
    w2_load.start()

    barrier = pltpu.get_barrier_semaphore()

    def greet(device):
        pl.semaphore_signal(barrier, inc=1, device_id=device, device_id_type=pl.DeviceIdType.MESH)

    greet({"bricks": below})
    greet({"bricks": above})
    for j in range(1, nq):
        greet(chip_at(j))
    for j in range(1, ns):
        greet(scene_at(j))

    eye256 = eye(PL, PL)
    eye128 = eye(L, L)
    eye64 = eye(C, C)
    eye64w = eye(C, L)

    def load_features(column):
        bx, by = column // 2, column % 2
        for bz in range(2):
            n = column * 2 + bz
            live = mask[0, n : n + 1, :].astype(F32)
            live = jnp.broadcast_to(live, (L, 2 * PL)).astype(BF16)
            masked = feat[0, n] * live[:C]
            for h in range(2):
                cols = slice(h * PL, (h + 1) * PL)
                stack = jnp.concatenate([masked[:, cols], masked[:, cols], live[:, cols]], axis=0)
                turned = dot_nt(eye256, stack)
                x, y, z = bx * E + 4 * h, by * E, bz * E
                place = (slice(x, x + 4), slice(y, y + E), slice(z, z + E))
                u0[place] = turned[:, :L].reshape(4, E, E, L)
                mm[place] = turned[:, L:].reshape(4, E, E, L)

    def load_cotangent(column):
        bx, by = column // 2, column % 2
        for bz in range(2):
            value = cot[0, column * 2 + bz]
            for h in range(2):
                cols = slice(h * PL, (h + 1) * PL)
                stack = jnp.concatenate([value[:, cols], value[:, cols]], axis=0)
                x, y, z = bx * E + 4 * h, by * E, bz * E
                place = (slice(x, x + 4), slice(y, y + E), slice(z, z + E))
                ct[place] = dot_nt(eye256, stack).reshape(4, E, E, L)

    def store_bricks(oo, target):
        for n in range(8):
            bx, by, bz = n // 4, n // 2 % 2, n % 2
            rows = oo[bx * E : bx * E + E, by * E : by * E + E, bz * E : bz * E + E, :]
            rows = rows.reshape(E * E * E, L).astype(BF16)
            target[0, n] = dot_nt(eye64w, rows).astype(BF16)

    def prepare_weights(w, number, forward):
        spread = jnp.concatenate([eye64, eye64], axis=1)
        for m in range(14):
            size = L if m < 13 else C
            tile = w[:, m * L : m * L + size]
            if forward:
                twice = jnp.concatenate([tile, tile], axis=0)
                wt[m * L : m * L + size, :] = dot_nt(eye128 if m < 13 else eye64, twice)
            else:
                for part in range(size // C):
                    zeros = jnp.zeros((C, L), BF16)
                    if m == 13:
                        select = spread
                    else:
                        select = jnp.concatenate([spread, zeros] if part == 0 else [zeros, spread], axis=0)
                    k = 2 * m + part
                    wd[k * C : k * C + C, :] = dot_nn(tile, select)
        low = low_lanes(C)
        for dy in (-1, 0, 1):
            for i, dz in enumerate((-1, 0, 1)):

                def block(dx):
                    if forward:
                        k = tap_of(dx, dy, dz)
                        return wt[k * C : k * C + C, :]
                    k = tap_of(-dx, -dy, -dz)
                    return wd[k * C : k * C + C, :]

                rows = slice((dy + 1) * PL + i * C, (dy + 1) * PL + i * C + C)
                wa[number, rows, :L] = jnp.where(low, block(-1), block(1)).astype(BF16)
                wa[number, rows, L:] = block(0).astype(BF16)
            wa[number, (dy + 1) * PL + 3 * C : (dy + 2) * PL, :] = jnp.zeros((C, PL), BF16)

    low_half = low_lanes(PL // 2)

    def halo_copy(field, way):
        return copy_to(
            halo_out.at[field, way],
            halo_in.at[field, way],
            halo_send.at[field, way],
            halo_recv.at[field, way],
            {"bricks": above if way == 0 else below},
        )

    def send_halo(field):
        for way, z in ((0, S - 1), (1, 0)):
            plane = us[pl.ds(z, PL, stride=S), :]
            packed = jnp.where(low_half, plane[: PL // 2], plane[PL // 2 :])
            halo_out[field, way] = packed.astype(BF16)
            halo_copy(field, way).start()

    def receive_halo(field):
        for way in range(2):
            halo_copy(field, way).wait_recv()
            got = halo_in[field, way].astype(F32)
            exists = (b > 0) if way == 0 else (b < nb - 1)
            got = got * jnp.where(exists, 1.0, 0.0)
            swapped = pltpu.roll(got, C, 1)
            halo_wide[field, way, : PL // 2, :] = jnp.where(low_half, got, swapped)
            halo_wide[field, way, PL // 2 :, :] = jnp.where(low_half, swapped, got)

    def add_halo(field, number):
        for way in range(2):
            plane = halo_wide[field, way]
            down = jnp.where(z_of == 0, 0.0, pltpu.roll(plane, 1, 0))
            up = jnp.where(z_of == S - 1, 0.0, pltpu.roll(plane, PL - 1, 0))
            rows = jnp.concatenate([jnp.where(low_plane, down, plane), up], axis=1).astype(BF16)
            taps = [wa[number, e * PL + 2 * C * way : e * PL + 2 * C * way + C, :] for e in range(3)]
            taps = jnp.concatenate(taps + [jnp.zeros((C, PL), BF16)], axis=0)
            got = dot_nn(rows, taps)
            edge = jnp.zeros((S, L), F32)
            left = jnp.concatenate([edge, got[: PL - S, :L]], axis=0)
            right = jnp.concatenate([got[S:, :L], edge], axis=0)
            sides = jnp.where(low_plane, left, right)
            added[way] = sides + pltpu.roll(sides, C, 1) + got[:, L:]

    low_plane = low_lanes(PL)
    z_of = lax.broadcasted_iota(jnp.int32, (PL, L), 0) & (S - 1)

    def rows_of(x):
        return slice(x * PL, x * PL + PL)

    def spread(ref, x):
        rows = ref[x * S : x * S + S, :]
        return jnp.broadcast_to(rows[:, None, :], (S, S, L)).reshape(PL, L)

    def fill(field, x, u):
        down = jnp.where(z_of == 0, 0.0, pltpu.roll(u, 1, 0))
        up = jnp.where(z_of == S - 1, 0.0, pltpu.roll(u, PL - 1, 0))
        tile = jnp.where(low_plane, down, u)
        field[x, 1 : S + 1, :, :L] = tile.reshape(S, S, L).astype(BF16)
        field[x, 1 : S + 1, :, L:] = up.reshape(S, S, L).astype(BF16)

    def fill_halo(field, number):
        below_at = (z_of == 0) & low_plane
        above_at = z_of == S - 1
        for x in range(S):
            tile = field[x, 1 : S + 1, :, :L].reshape(PL, L).astype(F32)
            tile = jnp.where(below_at, spread(halo_wide.at[number, 0], x), tile)
            field[x, 1 : S + 1, :, :L] = tile.reshape(S, S, L).astype(BF16)
            tile = field[x, 1 : S + 1, :, L:].reshape(PL, L).astype(F32)
            tile = jnp.where(above_at, spread(halo_wide.at[number, 1], x), tile)
            field[x, 1 : S + 1, :, L:] = tile.reshape(S, S, L).astype(BF16)

    def conv(field, number):
        for x in range(0, S, 4):
            rows = [field[x : x + 4, e : e + S].reshape(4 * PL, PL) for e in range(3)]
            product = dot_nn(jnp.concatenate(rows, axis=1), wa[number])
            yy[x + 1 : x + 1 + 4] = product.reshape(4, PL, PL)

    def conv_result(x):
        sides = jnp.where(low_plane, yy[x, :, :L], yy[x + 2, :, :L])
        outer = jnp.where(z_of == 0, spread(added.at[0], x), spread(added.at[1], x))
        outer = jnp.where((z_of == 0) | (z_of == S - 1), outer, 0.0)
        return sides + pltpu.roll(sides, C, 1) + yy[x + 1, :, L:] + outer

    def turn(x, value):
        gt[(x + 1) * C : (x + 2) * C, :] = dot_nt(eye64w, value).astype(BF16)

    def weight_grad(field, number):
        left = jnp.concatenate([gt[x * C : (x + 3) * C, :] for x in range(S)], axis=1)
        for e in range(3):
            grads[e] = dot_nn(left, field[:, e : e + S].reshape(S * PL, PL))
        low = low_lanes(96)
        for e in range(3):
            for j in range(3):
                row = e * 3 * C + j * C
                pack[number, row // HALF, row % HALF : row % HALF + C, :] = grads[e, j * C : j * C + C, :L]
            row = 9 * C + e * 96 - HALF
            pack[number, 1, row : row + 96, :] = jnp.where(low, grads[e, :96, L:], grads[e, 96:, L:])

    def pack_bias(number, total):
        row = jnp.sum(total, axis=0, keepdims=True)
        pack[number, 1, BIAS_ROW : BIAS_ROW + 1, :] = row

    chunk = HALF // nq

    def split_bias(value, first_row):
        row = lax.broadcasted_iota(jnp.int32, value.shape, 0) + first_row
        at = BIAS_ROW % chunk
        whole = value[at : at + 1] + value[at + 1 : at + 2]
        high = whole.astype(BF16).astype(F32)
        value = jnp.where(row == HALF + BIAS_ROW, high, value)
        return jnp.where(row == HALF + BIAS_ROW + 1, whole - high, value)

    def pair_copy(number, step):
        if step == 0:
            src, dst = pack.at[number, 1 - core], part1.at[number]
        else:
            src, dst = full.at[number, core], full.at[number, core]
        return copy_to(src, dst, pair_send.at[number, step], pair_recv.at[number, step], {"bricks": other})

    def reduce_chips_copy(number, j):
        return copy_to(
            sum1.at[number, chip_to(j)],
            part2.at[number, j],
            chip_send.at[number, 0, j],
            chip_recv.at[number, 0, j],
            chip_at(j),
        )

    def scene_copy(number, j, sender):
        return copy_to(
            sum2.at[number],
            part3.at[number, sender],
            scene_send.at[number, j],
            scene_recv.at[number, j],
            scene_at(j),
        )

    def gather_chips_copy(number, j, sender):
        return copy_to(
            sum3.at[number],
            full.at[number, core, sender],
            chip_send.at[number, 1, j],
            chip_recv.at[number, 1, j],
            chip_at(j),
        )

    def sum_start(number):
        pair_copy(number, 0).start()

    def sum_chips(number):
        pair_copy(number, 0).wait_recv()
        total = pack[number, core] + part1[number]
        sum1[number] = total.astype(BF16).reshape(nq, chunk, L)
        n = BIAS_ROW // chunk
        rows = split_bias(total[n * chunk : n * chunk + chunk], core * HALF + n * chunk)
        sum1[number, n] = rows.astype(BF16)
        for j in range(1, nq):
            reduce_chips_copy(number, j).start()

    def sum_scenes(number):
        for j in range(1, nq):
            reduce_chips_copy(number, j).wait_recv()
        total = sum1[number, q].astype(F32)
        for j in range(1, nq):
            total += part2[number, j].astype(F32)
        total = split_bias(total, core * HALF + q * chunk).astype(BF16)
        sum2[number] = total
        part3[number, s] = total
        for j in range(1, ns):
            scene_copy(number, j, s).start()

    def gather_chips(number):
        for j in range(1, ns):
            scene_copy(number, j, scene_from(j)).wait_recv()
        total = part3[number, 0].astype(F32)
        for j in range(1, ns):
            total += part3[number, j].astype(F32)
        total = split_bias(total, core * HALF + q * chunk).astype(BF16)
        sum3[number] = total
        full[number, core, q] = total
        for j in range(1, nq):
            gather_chips_copy(number, j, q).start()

    def gather_pair(number):
        for j in range(1, nq):
            gather_chips_copy(number, j, chip_from(j)).wait_recv()
        pair_copy(number, 1).start()

    def sum_end(number):
        pair_copy(number, 1).wait_recv()

    def sends_end(number):
        pair_copy(number, 0).wait_send()
        for j in range(1, nq):
            reduce_chips_copy(number, j).wait_send()
            gather_chips_copy(number, j, q).wait_send()
        for j in range(1, ns):
            scene_copy(number, j, s).wait_send()

    for field in (f0, f1, f2):
        field[:, 0] = jnp.zeros((S, S, PL), BF16)
        field[:, S + 1] = jnp.zeros((S, S, PL), BF16)
    yy[0] = jnp.zeros((PL, PL), F32)
    yy[S + 1] = jnp.zeros((PL, PL), F32)
    gt[:C] = jnp.zeros((C, PL), BF16)
    gt[(S + 1) * C :] = jnp.zeros((C, PL), BF16)
    for number in range(2):
        pack[number, 1, BIAS_ROW:, :] = jnp.zeros((HALF - BIAS_ROW, L), F32)

    for column in range(4):
        load_features(column)
    for x in range(S):
        us[rows_of(x), :] = u0[x].reshape(PL, L)
        fill(f0, x, u0[x].reshape(PL, L))
    pl.semaphore_wait(barrier, 2 + (nq - 1) + (ns - 1))
    send_halo(0)
    prepare_weights(w1, 0, True)
    conv(f0, 0)
    w2_load.wait()
    prepare_weights(w2, 1, True)
    prepare_weights(w2, 2, False)
    prepare_weights(w1, 3, False)
    cot_load.wait()
    for column in range(4):
        load_cotangent(column)
    receive_halo(0)
    add_halo(0, 0)

    def after_first(x):
        live = mm[x].reshape(PL, L)
        bias = jnp.concatenate([b1[...], b1[...]], axis=1)
        first = live * (conv_result(x) + bias)
        sig = sigmoid(first)
        hidden = first * sig
        sl[rows_of(x), :] = live * (sig + hidden * (1.0 - sig))
        hidden = hidden.astype(BF16).astype(F32)
        us[rows_of(x), :] = hidden
        fill(f1, x, hidden)

    for x in range(S):
        after_first(x)
    send_halo(1)
    conv(f1, 1)
    fill_halo(f0, 0)
    receive_halo(1)
    add_halo(1, 1)

    def after_second(x):
        live = mm[x].reshape(PL, L)
        bias = jnp.concatenate([b2[...], b2[...]], axis=1)
        summed = live * (conv_result(x) + bias) + u0[x].reshape(PL, L)
        sig = sigmoid(summed)
        value = summed * sig
        oo[x] = value.reshape(S, S, L)
        slope = sig + value * (1.0 - sig)
        grad = (ct[x].reshape(PL, L) * slope * live).astype(BF16)
        turn(x, grad)
        grad = grad.astype(F32)
        us[rows_of(x), :] = grad
        gs[rows_of(x), :] = grad
        fill(f2, x, grad)
        return jnp.sum(grad.reshape(PL // 8, 8, L), axis=0)

    total = jnp.zeros((8, L), F32)
    for x in range(S):
        total += after_second(x)
    send_halo(2)
    pack_bias(1, total)
    conv(f2, 2)
    fill_halo(f1, 1)
    weight_grad(f1, 1)
    sum_start(1)
    receive_halo(2)
    add_halo(2, 2)

    def after_third(x):
        grad = (conv_result(x) * sl[rows_of(x), :]).astype(BF16)
        turn(x, grad)
        grad = grad.astype(F32)
        us[rows_of(x), :] = grad
        fill(f2, x, grad)
        return jnp.sum(grad.reshape(PL // 8, 8, L), axis=0)

    total = jnp.zeros((8, L), F32)
    for x in range(S):
        total += after_third(x)
    send_halo(3)
    pack_bias(0, total)
    sum_chips(1)
    weight_grad(f0, 0)
    sum_start(0)
    store_bricks(oo, out)
    sum_chips(0)
    conv(f2, 3)
    sum_scenes(1)
    receive_halo(3)
    add_halo(3, 3)

    def after_fourth(x):
        value = mm[x].reshape(PL, L) * (gs[rows_of(x), :] + conv_result(x))
        o2[x] = value.reshape(S, S, L)

    for x in range(S):
        after_fourth(x)
    sum_scenes(0)
    gather_chips(1)
    store_bricks(o2, gfeat)
    gather_chips(0)
    for field in range(4):
        for way in range(2):
            halo_copy(field, way).wait_send()
    gather_pair(1)
    sends_end(1)
    sum_end(1)
    sums[1] = full[1].reshape(2, HALF, L)
    gather_pair(0)
    pair_copy(1, 1).wait_send()
    sends_end(0)
    sum_end(0)
    sums[0] = full[0].reshape(2, HALF, L)
    pair_copy(0, 1).wait_send()


def unpack(sums, number, weight, bias):
    low = low_lanes(C)

    def packed(row, size):
        return sums[number, row // HALF, row % HALF : row % HALF + size, :].astype(F32)

    def piece(k):
        dx, dy, dz = k // 9, k // 3 % 3, k % 3
        j = 2 - dx
        if dz < 2:
            return packed(dy * 3 * C + j * C, C), dz
        base = 9 * C + dy * 96
        if j == 0:
            return packed(base, C), 0
        if j == 2:
            return packed(base + 32, C), 1
        first = packed(base + 64, 32)
        second = pltpu.roll(packed(base, 32), C, 1)
        return jnp.concatenate([first, second], axis=0), 0

    def placed(k, half):
        value, at = piece(k)
        return value if at == half else pltpu.roll(value, C, 1)

    for m in range(13):
        weight[:, m * L : m * L + L] = jnp.where(low, placed(2 * m, 0), placed(2 * m + 1, 1))
    weight[:, 13 * L :] = placed(26, 0)[:, :C]
    rows = packed(HALF + BIAS_ROW, 16)
    bias[...] = (rows[0:1] + rows[1:2])[:, :C]


def finish(out_in, gfeat_in, sums, out, gfeat, gw1, gw2, gb1, gb2, sem):
    copies = [
        pltpu.make_async_copy(out_in, out, sem.at[0]),
        pltpu.make_async_copy(gfeat_in, gfeat, sem.at[1]),
    ]
    for copy in copies:
        copy.start()
    unpack(sums, 0, gw1, gb1)
    unpack(sums, 1, gw2, gb2)
    for copy in copies:
        copy.wait()


def local(nb, ns, features, cotangent, mask, w1, b1, w2, b2):
    nq = nb // 2
    chunk = HALF // nq
    vmem = pltpu.VMEM
    field = vmem((S, S + 2, S, PL), BF16)
    block4 = vmem((S, S, S, L), F32)
    block2 = vmem((S * PL, L), F32)
    dma = pltpu.SemaphoreType.DMA
    scratch = [
        vmem(features.shape, BF16),
        vmem(w2.shape, BF16),
        field,
        field,
        field,
        vmem((S + 2, PL, PL), F32),
        vmem(((S + 2) * C, PL), BF16),
        block4,
        block4,
        block4,
        block2,
        block2,
        block2,
        block4,
        block4,
        vmem((27 * C, L), F32),
        vmem((27 * C, L), F32),
        vmem((4, 3 * PL, PL), BF16),
        vmem((4, 2, PL // 2, L), BF16),
        vmem((4, 2, PL // 2, L), BF16),
        vmem((4, 2, PL, L), F32),
        vmem((2, PL, L), F32),
        vmem((3, 3 * C, PL), F32),
        vmem((2, 2, HALF, L), F32),
        vmem((2, HALF, L), F32),
        vmem((2, nq, chunk, L), BF16),
        vmem((2, nq, chunk, L), BF16),
        vmem((2, chunk, L), BF16),
        vmem((2, ns, chunk, L), BF16),
        vmem((2, chunk, L), BF16),
        vmem((2, 2, nq, chunk, L), BF16),
        dma((4, 2)),
        dma((4, 2)),
        dma((2, 2)),
        dma((2, 2)),
        dma((2, 2, nq)),
        dma((2, 2, nq)),
        dma((2, ns)),
        dma((2, ns)),
        dma((2,)),
    ]
    shape = jax.ShapeDtypeStruct
    in_vmem = pl.BlockSpec(memory_space=pltpu.VMEM)
    anywhere = pl.BlockSpec(memory_space=pl.ANY)
    output, grad_features, sums = pl.pallas_call(
        functools.partial(kernel, nb, ns),
        out_shape=[
            pltpu.VMEM(features.shape, BF16),
            pltpu.VMEM(features.shape, BF16),
            pltpu.VMEM((2, 2, HALF, L), BF16),
        ],
        in_specs=[in_vmem, anywhere, in_vmem, in_vmem, in_vmem, anywhere, in_vmem],
        out_specs=[in_vmem] * 3,
        scratch_shapes=scratch,
        compiler_params=pltpu.CompilerParams(
            collective_id=0, has_side_effects=True, vmem_limit_bytes=56 * 1024 * 1024
        ),
        name="residual_block",
    )(features, cotangent, mask, w1, b1.reshape(1, C), w2, b2.reshape(1, C))
    output, grad_features, gw1, gw2, gb1, gb2 = pl.pallas_call(
        finish,
        out_shape=[
            shape(features.shape, BF16),
            shape(features.shape, BF16),
            shape(w1.shape, F32),
            shape(w2.shape, F32),
            shape((1, C), F32),
            shape((1, C), F32),
        ],
        in_specs=[in_vmem] * 3,
        out_specs=[anywhere] * 2 + [in_vmem] * 4,
        scratch_shapes=[dma((2,))],
        compiler_params=pltpu.CompilerParams(vmem_limit_bytes=8 * 1024 * 1024),
        name="finish",
    )(output, grad_features, sums)
    return output, grad_features, gw1, gw2, gb1.reshape(C), gb2.reshape(C)


def solution(mesh):
    nb, ns = mesh.shape["bricks"], mesh.shape["scenes"]

    def program(features, cotangent, neighbours, mask, weight_one, bias_one, weight_two, bias_two):
        del neighbours
        split = P("scenes", "bricks", None, None)
        return jax.shard_map(
            functools.partial(local, nb, ns),
            mesh=mesh,
            in_specs=(split, split, P("scenes", "bricks", None), P(), P(), P(), P()),
            out_specs=(split, split, P(), P(), P(), P()),
            check_vma=False,
        )(features, cotangent, mask, weight_one, bias_one, weight_two, bias_two)

    return program
```

```python
import functools

import jax
import jax.numpy as jnp
from jax import lax
from jax.experimental import pallas as pl
from jax.experimental.pallas import tpu as pltpu
from jax.sharding import PartitionSpec as P

C = 64
E = 8
S = 16
PL = S * S
L = 128
HALF = 512
BIAS_ROW = 864 - HALF
F32 = jnp.float32
BF16 = jnp.bfloat16


def dot_nn(a, b):
    return lax.dot_general(a, b, (((1,), (0,)), ((), ())), preferred_element_type=F32)


def dot_nt(a, b):
    return lax.dot_general(a, b, (((1,), (1,)), ((), ())), preferred_element_type=F32)


def eye(rows, cols):
    r = lax.broadcasted_iota(jnp.int32, (rows, cols), 0)
    c = lax.broadcasted_iota(jnp.int32, (rows, cols), 1)
    return jnp.where(r == c, 1.0, 0.0).astype(BF16)


def low_lanes(rows):
    return lax.broadcasted_iota(jnp.int32, (rows, L), 1) < C


def tap_of(dx, dy, dz):
    return 9 * (dx + 1) + 3 * (dy + 1) + (dz + 1)


def copy_to(src, dst, send, recv, device):
    return pltpu.make_async_remote_copy(
        src_ref=src,
        dst_ref=dst,
        send_sem=send,
        recv_sem=recv,
        device_id=device,
        device_id_type=pl.DeviceIdType.MESH,
    )


def sigmoid(v):
    return 1.0 / (1.0 + jnp.exp(-v))


def kernel(
    nb,
    ns,
    feat_hbm,
    cot_hbm,
    mask_hbm,
    w1_hbm,
    b1_hbm,
    w2_hbm,
    b2_hbm,
    out,
    gfeat,
    sums,
    cot,
    w2,
    feat,
    mask,
    w1,
    b1,
    b2,
    f0,
    f1,
    f2,
    yy,
    gt,
    u0,
    mm,
    ct,
    us,
    sl,
    gs,
    oo,
    o2,
    wt,
    wd,
    wa,
    halo_out,
    halo_in,
    halo_wide,
    added,
    grads,
    pack,
    part1,
    sum1,
    part2,
    sum2,
    part3,
    sum3,
    full,
    halo_send,
    halo_recv,
    pair_send,
    pair_recv,
    chip_send,
    chip_recv,
    scene_send,
    scene_recv,
    load_sem,
):
    nq = nb // 2
    b = lax.axis_index("bricks")
    s = lax.axis_index("scenes")
    core = lax.rem(b, 2)
    q = b // 2
    below = lax.rem(b + nb - 1, nb)
    above = lax.rem(b + 1, nb)
    other = b + 1 - 2 * core

    nx = 4 if nq % 4 == 0 else nq
    ny = nq // nx
    cx, cy = lax.rem(q, nx), q // nx

    def far(step, size):
        return min(step, size - step)

    chip_steps = [(dy, dx) for dy in range(ny) for dx in range(nx)][1:]
    chip_steps = [None] + sorted(chip_steps, key=lambda t: -far(t[0], ny) - far(t[1], nx))
    scene_steps = [None] + sorted(range(1, ns), key=lambda t: -far(t, ns))

    def chip_to(j):
        dy, dx = chip_steps[j]
        return lax.rem(cy + dy, ny) * nx + lax.rem(cx + dx, nx)

    def chip_from(j):
        dy, dx = chip_steps[j]
        return lax.rem(cy + ny - dy, ny) * nx + lax.rem(cx + nx - dx, nx)

    def chip_at(j):
        return {"bricks": 2 * chip_to(j) + core}

    def scene_at(j):
        return {"scenes": lax.rem(s + scene_steps[j], ns)}

    def scene_from(j):
        return lax.rem(s + ns - scene_steps[j], ns)

    cot_load = pltpu.make_async_copy(cot_hbm, cot, load_sem.at[0])
    w2_load = pltpu.make_async_copy(w2_hbm, w2, load_sem.at[1])
    feat_load = pltpu.make_async_copy(feat_hbm, feat, load_sem.at[2])
    mask_load = pltpu.make_async_copy(mask_hbm, mask, load_sem.at[3])
    w1_load = pltpu.make_async_copy(w1_hbm, w1, load_sem.at[4])
    b1_load = pltpu.make_async_copy(b1_hbm, b1, load_sem.at[5])
    b2_load = pltpu.make_async_copy(b2_hbm, b2, load_sem.at[6])
    feat_load.start()
    mask_load.start()

    barrier = pltpu.get_barrier_semaphore()

    def greet(device):
        pl.semaphore_signal(barrier, inc=1, device_id=device, device_id_type=pl.DeviceIdType.MESH)

    greet({"bricks": below})
    greet({"bricks": above})
    for j in range(1, nq):
        greet(chip_at(j))
    for j in range(1, ns):
        greet(scene_at(j))

    for load in (w1_load, w2_load, b1_load, b2_load, cot_load):
        load.start()

    eye256 = eye(PL, PL)
    eye128 = eye(L, L)
    eye64 = eye(C, C)
    eye64w = eye(C, L)

    def load_features(column):
        bx, by = column // 2, column % 2
        for bz in range(2):
            n = column * 2 + bz
            live = mask[0, n : n + 1, :].astype(F32)
            live = jnp.broadcast_to(live, (L, 2 * PL)).astype(BF16)
            masked = feat[0, n] * live[:C]
            for h in range(2):
                cols = slice(h * PL, (h + 1) * PL)
                stack = jnp.concatenate([masked[:, cols], masked[:, cols], live[:, cols]], axis=0)
                turned = dot_nt(eye256, stack)
                x, y, z = bx * E + 4 * h, by * E, bz * E
                place = (slice(x, x + 4), slice(y, y + E), slice(z, z + E))
                u0[place] = turned[:, :L].reshape(4, E, E, L)
                mm[place] = turned[:, L:].reshape(4, E, E, L)

    def load_cotangent(column):
        bx, by = column // 2, column % 2
        for bz in range(2):
            value = cot[0, column * 2 + bz]
            for h in range(2):
                cols = slice(h * PL, (h + 1) * PL)
                stack = jnp.concatenate([value[:, cols], value[:, cols]], axis=0)
                x, y, z = bx * E + 4 * h, by * E, bz * E
                place = (slice(x, x + 4), slice(y, y + E), slice(z, z + E))
                ct[place] = dot_nt(eye256, stack).reshape(4, E, E, L)

    def store_bricks(oo, target):
        for n in range(8):
            bx, by, bz = n // 4, n // 2 % 2, n % 2
            rows = oo[bx * E : bx * E + E, by * E : by * E + E, bz * E : bz * E + E, :]
            rows = rows.reshape(E * E * E, L).astype(BF16)
            target[0, n] = dot_nt(eye64w, rows).astype(BF16)

    def prepare_weights(w, number, forward):
        spread = jnp.concatenate([eye64, eye64], axis=1)
        for m in range(14):
            size = L if m < 13 else C
            tile = w[:, m * L : m * L + size]
            if forward:
                twice = jnp.concatenate([tile, tile], axis=0)
                wt[m * L : m * L + size, :] = dot_nt(eye128 if m < 13 else eye64, twice)
            else:
                for part in range(size // C):
                    zeros = jnp.zeros((C, L), BF16)
                    if m == 13:
                        select = spread
                    else:
                        select = jnp.concatenate([spread, zeros] if part == 0 else [zeros, spread], axis=0)
                    k = 2 * m + part
                    wd[k * C : k * C + C, :] = dot_nn(tile, select)
        low = low_lanes(C)
        for dy in (-1, 0, 1):
            for i, dz in enumerate((-1, 0, 1)):

                def block(dx):
                    if forward:
                        k = tap_of(dx, dy, dz)
                        return wt[k * C : k * C + C, :]
                    k = tap_of(-dx, -dy, -dz)
                    return wd[k * C : k * C + C, :]

                rows = slice((dy + 1) * PL + i * C, (dy + 1) * PL + i * C + C)
                wa[number, rows, :L] = jnp.where(low, block(-1), block(1)).astype(BF16)
                wa[number, rows, L:] = block(0).astype(BF16)
            wa[number, (dy + 1) * PL + 3 * C : (dy + 2) * PL, :] = jnp.zeros((C, PL), BF16)

    low_half = low_lanes(PL // 2)

    def halo_copy(field, way):
        return copy_to(
            halo_out.at[field, way],
            halo_in.at[field, way],
            halo_send.at[field, way],
            halo_recv.at[field, way],
            {"bricks": above if way == 0 else below},
        )

    def send_halo(field):
        for way, z in ((0, S - 1), (1, 0)):
            plane = us[pl.ds(z, PL, stride=S), :]
            packed = jnp.where(low_half, plane[: PL // 2], plane[PL // 2 :])
            halo_out[field, way] = packed.astype(BF16)
            halo_copy(field, way).start()

    def receive_halo(field):
        for way in range(2):
            halo_copy(field, way).wait_recv()
            got = halo_in[field, way].astype(F32)
            exists = (b > 0) if way == 0 else (b < nb - 1)
            got = got * jnp.where(exists, 1.0, 0.0)
            swapped = pltpu.roll(got, C, 1)
            halo_wide[field, way, : PL // 2, :] = jnp.where(low_half, got, swapped)
            halo_wide[field, way, PL // 2 :, :] = jnp.where(low_half, swapped, got)

    def add_halo(field, number):
        for way in range(2):
            plane = halo_wide[field, way]
            down = jnp.where(z_of == 0, 0.0, pltpu.roll(plane, 1, 0))
            up = jnp.where(z_of == S - 1, 0.0, pltpu.roll(plane, PL - 1, 0))
            rows = jnp.concatenate([jnp.where(low_plane, down, plane), up], axis=1).astype(BF16)
            taps = [wa[number, e * PL + 2 * C * way : e * PL + 2 * C * way + C, :] for e in range(3)]
            taps = jnp.concatenate(taps + [jnp.zeros((C, PL), BF16)], axis=0)
            got = dot_nn(rows, taps)
            edge = jnp.zeros((S, L), F32)
            left = jnp.concatenate([edge, got[: PL - S, :L]], axis=0)
            right = jnp.concatenate([got[S:, :L], edge], axis=0)
            sides = jnp.where(low_plane, left, right)
            added[way] = sides + pltpu.roll(sides, C, 1) + got[:, L:]

    low_plane = low_lanes(PL)
    z_of = lax.broadcasted_iota(jnp.int32, (PL, L), 0) & (S - 1)

    def rows_of(x):
        return slice(x * PL, x * PL + PL)

    def spread(ref, x):
        rows = ref[x * S : x * S + S, :]
        return jnp.broadcast_to(rows[:, None, :], (S, S, L)).reshape(PL, L)

    def fill(field, x, u):
        down = jnp.where(z_of == 0, 0.0, pltpu.roll(u, 1, 0))
        up = jnp.where(z_of == S - 1, 0.0, pltpu.roll(u, PL - 1, 0))
        tile = jnp.where(low_plane, down, u)
        field[x, 1 : S + 1, :, :L] = tile.reshape(S, S, L).astype(BF16)
        field[x, 1 : S + 1, :, L:] = up.reshape(S, S, L).astype(BF16)

    def fill_halo(field, number):
        below_at = (z_of == 0) & low_plane
        above_at = z_of == S - 1
        for x in range(S):
            tile = field[x, 1 : S + 1, :, :L].reshape(PL, L).astype(F32)
            tile = jnp.where(below_at, spread(halo_wide.at[number, 0], x), tile)
            field[x, 1 : S + 1, :, :L] = tile.reshape(S, S, L).astype(BF16)
            tile = field[x, 1 : S + 1, :, L:].reshape(PL, L).astype(F32)
            tile = jnp.where(above_at, spread(halo_wide.at[number, 1], x), tile)
            field[x, 1 : S + 1, :, L:] = tile.reshape(S, S, L).astype(BF16)

    def conv(field, number):
        for x in range(0, S, 4):
            rows = [field[x : x + 4, e : e + S].reshape(4 * PL, PL) for e in range(3)]
            product = dot_nn(jnp.concatenate(rows, axis=1), wa[number])
            yy[x + 1 : x + 1 + 4] = product.reshape(4, PL, PL)

    def conv_result(x):
        sides = jnp.where(low_plane, yy[x, :, :L], yy[x + 2, :, :L])
        outer = jnp.where(z_of == 0, spread(added.at[0], x), spread(added.at[1], x))
        outer = jnp.where((z_of == 0) | (z_of == S - 1), outer, 0.0)
        return sides + pltpu.roll(sides, C, 1) + yy[x + 1, :, L:] + outer

    def turn(x, value):
        gt[(x + 1) * C : (x + 2) * C, :] = dot_nt(eye64w, value).astype(BF16)

    def weight_grad(field, number):
        left = jnp.concatenate([gt[x * C : (x + 3) * C, :] for x in range(S)], axis=1)
        for e in range(3):
            grads[e] = dot_nn(left, field[:, e : e + S].reshape(S * PL, PL))
        low = low_lanes(96)
        for e in range(3):
            for j in range(3):
                row = e * 3 * C + j * C
                pack[number, row // HALF, row % HALF : row % HALF + C, :] = grads[e, j * C : j * C + C, :L]
            row = 9 * C + e * 96 - HALF
            pack[number, 1, row : row + 96, :] = jnp.where(low, grads[e, :96, L:], grads[e, 96:, L:])

    def pack_bias(number, total):
        row = jnp.sum(total, axis=0, keepdims=True)
        pack[number, 1, BIAS_ROW : BIAS_ROW + 1, :] = row

    chunk = HALF // nq

    def split_bias(value, first_row):
        row = lax.broadcasted_iota(jnp.int32, value.shape, 0) + first_row
        at = BIAS_ROW % chunk
        whole = value[at : at + 1] + value[at + 1 : at + 2]
        high = whole.astype(BF16).astype(F32)
        value = jnp.where(row == HALF + BIAS_ROW, high, value)
        return jnp.where(row == HALF + BIAS_ROW + 1, whole - high, value)

    def pair_copy(number, step):
        if step == 0:
            src, dst = pack.at[number, 1 - core], part1.at[number]
        else:
            src, dst = full.at[number, core], full.at[number, core]
        return copy_to(src, dst, pair_send.at[number, step], pair_recv.at[number, step], {"bricks": other})

    def reduce_chips_copy(number, j):
        return copy_to(
            sum1.at[number, chip_to(j)],
            part2.at[number, j],
            chip_send.at[number, 0, j],
            chip_recv.at[number, 0, j],
            chip_at(j),
        )

    def scene_copy(number, j, sender):
        return copy_to(
            sum2.at[number],
            part3.at[number, sender],
            scene_send.at[number, j],
            scene_recv.at[number, j],
            scene_at(j),
        )

    def gather_chips_copy(number, j, sender):
        return copy_to(
            sum3.at[number],
            full.at[number, core, sender],
            chip_send.at[number, 1, j],
            chip_recv.at[number, 1, j],
            chip_at(j),
        )

    def sum_start(number):
        pair_copy(number, 0).start()

    def sum_chips(number):
        pair_copy(number, 0).wait_recv()
        total = pack[number, core] + part1[number]
        sum1[number] = total.astype(BF16).reshape(nq, chunk, L)
        n = BIAS_ROW // chunk
        rows = split_bias(total[n * chunk : n * chunk + chunk], core * HALF + n * chunk)
        sum1[number, n] = rows.astype(BF16)
        for j in range(1, nq):
            reduce_chips_copy(number, j).start()

    def sum_scenes(number):
        for j in range(1, nq):
            reduce_chips_copy(number, j).wait_recv()
        total = sum1[number, q].astype(F32)
        for j in range(1, nq):
            total += part2[number, j].astype(F32)
        total = split_bias(total, core * HALF + q * chunk).astype(BF16)
        sum2[number] = total
        part3[number, s] = total
        for j in range(1, ns):
            scene_copy(number, j, s).start()

    def gather_chips(number):
        for j in range(1, ns):
            scene_copy(number, j, scene_from(j)).wait_recv()
        total = part3[number, 0].astype(F32)
        for j in range(1, ns):
            total += part3[number, j].astype(F32)
        total = split_bias(total, core * HALF + q * chunk).astype(BF16)
        sum3[number] = total
        full[number, core, q] = total
        for j in range(1, nq):
            gather_chips_copy(number, j, q).start()

    def gather_pair(number):
        for j in range(1, nq):
            gather_chips_copy(number, j, chip_from(j)).wait_recv()
        pair_copy(number, 1).start()

    def sum_end(number):
        pair_copy(number, 1).wait_recv()

    def sends_end(number):
        pair_copy(number, 0).wait_send()
        for j in range(1, nq):
            reduce_chips_copy(number, j).wait_send()
            gather_chips_copy(number, j, q).wait_send()
        for j in range(1, ns):
            scene_copy(number, j, s).wait_send()

    for field in (f0, f1, f2):
        field[:, 0] = jnp.zeros((S, S, PL), BF16)
        field[:, S + 1] = jnp.zeros((S, S, PL), BF16)
    yy[0] = jnp.zeros((PL, PL), F32)
    yy[S + 1] = jnp.zeros((PL, PL), F32)
    gt[:C] = jnp.zeros((C, PL), BF16)
    gt[(S + 1) * C :] = jnp.zeros((C, PL), BF16)
    for number in range(2):
        pack[number, 1, BIAS_ROW:, :] = jnp.zeros((HALF - BIAS_ROW, L), F32)

    feat_load.wait()
    mask_load.wait()
    for column in range(4):
        load_features(column)
    for x in range(S):
        us[rows_of(x), :] = u0[x].reshape(PL, L)
        fill(f0, x, u0[x].reshape(PL, L))
    pl.semaphore_wait(barrier, 2 + (nq - 1) + (ns - 1))
    send_halo(0)
    w1_load.wait()
    prepare_weights(w1, 0, True)
    conv(f0, 0)
    w2_load.wait()
    b1_load.wait()
    b2_load.wait()
    prepare_weights(w2, 1, True)
    prepare_weights(w2, 2, False)
    prepare_weights(w1, 3, False)
    cot_load.wait()
    for column in range(4):
        load_cotangent(column)
    receive_halo(0)
    add_halo(0, 0)

    def after_first(x):
        live = mm[x].reshape(PL, L)
        bias = jnp.concatenate([b1[...], b1[...]], axis=1)
        first = live * (conv_result(x) + bias)
        sig = sigmoid(first)
        hidden = first * sig
        sl[rows_of(x), :] = live * (sig + hidden * (1.0 - sig))
        hidden = hidden.astype(BF16).astype(F32)
        us[rows_of(x), :] = hidden
        fill(f1, x, hidden)

    for x in range(S):
        after_first(x)
    send_halo(1)
    conv(f1, 1)
    fill_halo(f0, 0)
    receive_halo(1)
    add_halo(1, 1)

    def after_second(x):
        live = mm[x].reshape(PL, L)
        bias = jnp.concatenate([b2[...], b2[...]], axis=1)
        summed = live * (conv_result(x) + bias) + u0[x].reshape(PL, L)
        sig = sigmoid(summed)
        value = summed * sig
        oo[x] = value.reshape(S, S, L)
        slope = sig + value * (1.0 - sig)
        grad = (ct[x].reshape(PL, L) * slope * live).astype(BF16)
        turn(x, grad)
        grad = grad.astype(F32)
        us[rows_of(x), :] = grad
        gs[rows_of(x), :] = grad
        fill(f2, x, grad)
        return jnp.sum(grad.reshape(PL // 8, 8, L), axis=0)

    total = jnp.zeros((8, L), F32)
    for x in range(S):
        total += after_second(x)
    send_halo(2)
    pack_bias(1, total)
    conv(f2, 2)
    fill_halo(f1, 1)
    weight_grad(f1, 1)
    sum_start(1)
    receive_halo(2)
    add_halo(2, 2)

    def after_third(x):
        grad = (conv_result(x) * sl[rows_of(x), :]).astype(BF16)
        turn(x, grad)
        grad = grad.astype(F32)
        us[rows_of(x), :] = grad
        fill(f2, x, grad)
        return jnp.sum(grad.reshape(PL // 8, 8, L), axis=0)

    total = jnp.zeros((8, L), F32)
    for x in range(S):
        total += after_third(x)
    send_halo(3)
    pack_bias(0, total)
    sum_chips(1)
    weight_grad(f0, 0)
    sum_start(0)
    store_bricks(oo, out)
    sum_chips(0)
    conv(f2, 3)
    sum_scenes(1)
    receive_halo(3)
    add_halo(3, 3)

    def after_fourth(x):
        value = mm[x].reshape(PL, L) * (gs[rows_of(x), :] + conv_result(x))
        o2[x] = value.reshape(S, S, L)

    for x in range(S):
        after_fourth(x)
    sum_scenes(0)
    gather_chips(1)
    store_bricks(o2, gfeat)
    gather_chips(0)
    for field in range(4):
        for way in range(2):
            halo_copy(field, way).wait_send()
    gather_pair(1)
    sends_end(1)
    sum_end(1)
    sums[1] = full[1].reshape(2, HALF, L)
    gather_pair(0)
    pair_copy(1, 1).wait_send()
    sends_end(0)
    sum_end(0)
    sums[0] = full[0].reshape(2, HALF, L)
    pair_copy(0, 1).wait_send()


def unpack(sums, number, weight, bias):
    low = low_lanes(C)

    def packed(row, size):
        return sums[number, row // HALF, row % HALF : row % HALF + size, :].astype(F32)

    def piece(k):
        dx, dy, dz = k // 9, k // 3 % 3, k % 3
        j = 2 - dx
        if dz < 2:
            return packed(dy * 3 * C + j * C, C), dz
        base = 9 * C + dy * 96
        if j == 0:
            return packed(base, C), 0
        if j == 2:
            return packed(base + 32, C), 1
        first = packed(base + 64, 32)
        second = pltpu.roll(packed(base, 32), C, 1)
        return jnp.concatenate([first, second], axis=0), 0

    def placed(k, half):
        value, at = piece(k)
        return value if at == half else pltpu.roll(value, C, 1)

    for m in range(13):
        weight[:, m * L : m * L + L] = jnp.where(low, placed(2 * m, 0), placed(2 * m + 1, 1))
    weight[:, 13 * L :] = placed(26, 0)[:, :C]
    rows = packed(HALF + BIAS_ROW, 16)
    bias[...] = (rows[0:1] + rows[1:2])[:, :C]


def finish(out_in, gfeat_in, sums, out, gfeat, gw1, gw2, gb1, gb2, sem):
    copies = [
        pltpu.make_async_copy(out_in, out, sem.at[0]),
        pltpu.make_async_copy(gfeat_in, gfeat, sem.at[1]),
    ]
    for copy in copies:
        copy.start()
    unpack(sums, 0, gw1, gb1)
    unpack(sums, 1, gw2, gb2)
    for copy in copies:
        copy.wait()


def local(nb, ns, features, cotangent, mask, w1, b1, w2, b2):
    nq = nb // 2
    chunk = HALF // nq
    vmem = pltpu.VMEM
    field = vmem((S, S + 2, S, PL), BF16)
    block4 = vmem((S, S, S, L), F32)
    block2 = vmem((S * PL, L), F32)
    dma = pltpu.SemaphoreType.DMA
    scratch = [
        vmem(features.shape, BF16),
        vmem(w2.shape, BF16),
        vmem(features.shape, BF16),
        vmem(mask.shape, jnp.int32),
        vmem(w1.shape, BF16),
        vmem((1, C), F32),
        vmem((1, C), F32),
        field,
        field,
        field,
        vmem((S + 2, PL, PL), F32),
        vmem(((S + 2) * C, PL), BF16),
        block4,
        block4,
        block4,
        block2,
        block2,
        block2,
        block4,
        block4,
        vmem((27 * C, L), F32),
        vmem((27 * C, L), F32),
        vmem((4, 3 * PL, PL), BF16),
        vmem((4, 2, PL // 2, L), BF16),
        vmem((4, 2, PL // 2, L), BF16),
        vmem((4, 2, PL, L), F32),
        vmem((2, PL, L), F32),
        vmem((3, 3 * C, PL), F32),
        vmem((2, 2, HALF, L), F32),
        vmem((2, HALF, L), F32),
        vmem((2, nq, chunk, L), BF16),
        vmem((2, nq, chunk, L), BF16),
        vmem((2, chunk, L), BF16),
        vmem((2, ns, chunk, L), BF16),
        vmem((2, chunk, L), BF16),
        vmem((2, 2, nq, chunk, L), BF16),
        dma((4, 2)),
        dma((4, 2)),
        dma((2, 2)),
        dma((2, 2)),
        dma((2, 2, nq)),
        dma((2, 2, nq)),
        dma((2, ns)),
        dma((2, ns)),
        dma((7,)),
    ]
    shape = jax.ShapeDtypeStruct
    in_vmem = pl.BlockSpec(memory_space=pltpu.VMEM)
    anywhere = pl.BlockSpec(memory_space=pl.ANY)
    output, grad_features, sums = pl.pallas_call(
        functools.partial(kernel, nb, ns),
        out_shape=[
            pltpu.VMEM(features.shape, BF16),
            pltpu.VMEM(features.shape, BF16),
            pltpu.VMEM((2, 2, HALF, L), BF16),
        ],
        in_specs=[anywhere] * 7,
        out_specs=[in_vmem] * 3,
        scratch_shapes=scratch,
        compiler_params=pltpu.CompilerParams(
            collective_id=0, has_side_effects=True, vmem_limit_bytes=56 * 1024 * 1024
        ),
        name="residual_block",
    )(features, cotangent, mask, w1, b1.reshape(1, C), w2, b2.reshape(1, C))
    output, grad_features, gw1, gw2, gb1, gb2 = pl.pallas_call(
        finish,
        out_shape=[
            shape(features.shape, BF16),
            shape(features.shape, BF16),
            shape(w1.shape, F32),
            shape(w2.shape, F32),
            shape((1, C), F32),
            shape((1, C), F32),
        ],
        in_specs=[in_vmem] * 3,
        out_specs=[anywhere] * 2 + [in_vmem] * 4,
        scratch_shapes=[dma((2,))],
        compiler_params=pltpu.CompilerParams(vmem_limit_bytes=8 * 1024 * 1024),
        name="finish",
    )(output, grad_features, sums)
    return output, grad_features, gw1, gw2, gb1.reshape(C), gb2.reshape(C)


def solution(mesh):
    nb, ns = mesh.shape["bricks"], mesh.shape["scenes"]

    def program(features, cotangent, neighbours, mask, weight_one, bias_one, weight_two, bias_two):
        del neighbours
        split = P("scenes", "bricks", None, None)
        return jax.shard_map(
            functools.partial(local, nb, ns),
            mesh=mesh,
            in_specs=(split, split, P("scenes", "bricks", None), P(), P(), P(), P()),
            out_specs=(split, split, P(), P(), P(), P()),
            check_vma=False,
        )(features, cotangent, mask, weight_one, bias_one, weight_two, bias_two)

    return program
```
